32 devices in a mesh: member: 4 (over z), patch: 4 (over y, x), level: 2 (over core).
Axes of the slice: x: 2, y: 2, z: 4, core: 2. Of those that a mesh axis runs over, the one named last changes fastest.
Arguments:
- ensemble: bfloat16 [256, 4, 4, 2, 12, 1024], P('member', 'patch', None, 'level'), may hold values from -6 to 6
- observations: float32 [4, 4, 2, 128], P('patch', 'member'), may hold values from -9 to 9
- precision: float32 [4, 4, 2, 128], P('patch', 'member'), may hold values from 0.25 to 4
- valid_count: int32 [4, 4, 2], P('patch', 'member'), may hold values from 16 to 128, as said below
- position: int32 [4, 4, 2, 128], P('patch', 'member'), may hold values from 0 to 12287
- level_kernel: float32 [2, 12], P('level'), may hold values from -4 to 4
- listed_blocks: int32 [4, 4, 8], P('patch', 'member'), may hold values from 0 to 17, as said below
Outputs:
- analysis: bfloat16 [256, 4, 4, 2, 12, 1024], P('member', 'patch', None, 'level')
The draws below stay inside these ranges and needn't reach their ends.
Inputs may be any that keep to these rules, and one draw needn't show every extreme that they name: `valid_count`: the valid observations of a block are its first slots; some block is full and some holds 16. `listed_blocks`: the entries of one patch are distinct, include both of the patch's own blocks (candidates 8 and 9), and name only patches inside the grid.
All inputs are finite; a program needn't handle non-finite values.
Results may differ from the reference program's by a relative error of at most 0.0082.
Values may be sent and summed in bfloat16 or wider, within the bound.
A program may use at most 128 MiB of HBM per device.

```python
import math
import jax
import jax.numpy as jnp
from jax import lax

MEMBERS = 256
VARIABLES = 12
COLUMNS = 1024
SLOTS = 128
OWN_BLOCKS = 2
LISTED = 8
SWEEPS = 6
LEVELS = 2
PATCH_ROWS = 4
PATCH_COLS = 4


def draw_valid_count(key, part):
    key = jax.random.fold_in(key, 5)
    counts = jax.random.randint(key, (PATCH_ROWS, PATCH_COLS, OWN_BLOCKS), SLOTS // 8, SLOTS + 1, dtype=jnp.int32)
    counts = counts.at[0, 0, 0].set(SLOTS)
    return counts.at[PATCH_ROWS - 1, PATCH_COLS - 1, OWN_BLOCKS - 1].set(SLOTS // 8)


def draw_listed_blocks(key, part):
    key = jax.random.fold_in(key, 9)
    total = 9 * OWN_BLOCKS
    grid_rows = jnp.arange(PATCH_ROWS, dtype=jnp.int32)[:, None, None]
    grid_cols = jnp.arange(PATCH_COLS, dtype=jnp.int32)[None, :, None]
    choices_all = jnp.arange(total, dtype=jnp.int32)[None, None, :]
    stepped = choices_all // OWN_BLOCKS
    row_shift = stepped // 3 - 1
    col_shift = stepped % 3 - 1
    inside = (grid_rows + row_shift >= 0) & (grid_rows + row_shift < PATCH_ROWS)
    inside = inside & (grid_cols + col_shift >= 0) & (grid_cols + col_shift < PATCH_COLS)
    centred = (row_shift == 0) & (col_shift == 0)
    noise = jax.random.randint(key, (PATCH_ROWS, PATCH_COLS, total), 0, 1 << 20, dtype=jnp.int32)
    scores = noise * 64 + choices_all + inside.astype(jnp.int32) * (1 << 27) + centred.astype(jnp.int32) * (1 << 28)
    return jax.lax.top_k(scores, LISTED)[1].astype(jnp.int32)


def plant(values, key, low, top_value):
    place = [jax.random.randint(jax.random.fold_in(key, axis), (), 0, length) for axis, length in enumerate(values.shape)]
    longest = values.shape.index(max(values.shape))
    neighbour = place[:longest] + [(place[longest] + 1) % values.shape[longest]] + place[longest + 1:]
    return values.at[tuple(place)].set(low).at[tuple(neighbour)].set(top_value)


def block_scale(rng, dims, shards, low, high):
    def one(dim, parts):
        heights = jax.random.uniform(jax.random.fold_in(jax.random.fold_in(rng, 6), dim), (parts,), jnp.float32, low / len(shards), high / len(shards))
        return jnp.repeat(jnp.exp(heights), dims[dim] // parts).reshape((-1,) + (1,) * (len(dims) - dim - 1))

    gain = one(*shards[0])
    for cut in shards[1:]:
        gain = gain * one(*cut)
    return gain


def normal_values(own_key, dims, spread, most, shards=(), held_as=jnp.bfloat16):
    entries = spread * jax.random.normal(own_key, dims, jnp.float32)
    if shards:
        entries = entries * block_scale(own_key, dims, shards, -0.22, 0.18)
    return jnp.clip(entries, -most, most).astype(held_as)


def setup_inputs(seed: int = 0) -> dict:
    splits = jax.random.split(jax.random.key(seed), 8)
    ensemble = normal_values(splits[0], (MEMBERS, PATCH_ROWS, PATCH_COLS, LEVELS, VARIABLES, COLUMNS), 1.0, 6.0, ((0, 4), (1, 4), (3, 2)))
    observations = normal_values(splits[1], (PATCH_ROWS, PATCH_COLS, OWN_BLOCKS, SLOTS), 1.5, 9.0, ((0, 4), (1, 4)), jnp.float32)
    precision = jnp.clip(jnp.exp(math.log(4.0) - 2.7725887 * jax.random.uniform(splits[2], (PATCH_ROWS, PATCH_COLS, OWN_BLOCKS, SLOTS), jnp.float32) ** block_scale(splits[2], (PATCH_ROWS, PATCH_COLS, OWN_BLOCKS, SLOTS), ((0, 4), (1, 4)), -0.2, 0.2)), 0.25, 4.0)
    valid_count = draw_valid_count(jax.random.fold_in(splits[7], 71), 0)
    position = plant(jax.random.randint(splits[4], (PATCH_ROWS, PATCH_COLS, OWN_BLOCKS, SLOTS), 0, VARIABLES * COLUMNS), jax.random.fold_in(splits[4], 1), 0, (VARIABLES * COLUMNS) - 1).astype(jnp.int32)
    level_kernel = normal_values(splits[5], (LEVELS, VARIABLES), 1.0, 4.0, ((0, 2),), jnp.float32)
    listed_blocks = draw_listed_blocks(jax.random.fold_in(splits[7], 71), 0)
    return {"ensemble": ensemble, "observations": observations, "precision": precision, "valid_count": valid_count, "position": position, "level_kernel": level_kernel, "listed_blocks": listed_blocks}


exact_precision = lax.Precision.HIGHEST

def taper_of(listed):
    stepped = listed // OWN_BLOCKS
    moved = jnp.abs(stepped // 3 - 1) + jnp.abs(stepped % 3 - 1)
    return jnp.where(moved == 0, 1.0, jnp.where(moved == 1, 0.6, 0.35)).astype(jnp.float32)

def analyse_patch(candidates, pairs, listed, fields):
    members = candidates.shape[0]
    chosen = jnp.take(candidates, listed, axis=1).reshape(members, LISTED * SLOTS)
    picked = jnp.take(pairs, listed, axis=1)
    tapering = taper_of(listed)
    widened = lax.optimization_barrier(chosen).astype(jnp.float32)
    centre = lax.optimization_barrier(jnp.mean(widened, axis=0))
    obs_pert = (widened - centre).astype(jnp.bfloat16)
    weight = (picked[1] * tapering[:, None]).reshape(LISTED * SLOTS)
    innovation = picked[0].reshape(LISTED * SLOTS) - centre
    pert_wide = lax.optimization_barrier(obs_pert).astype(jnp.float32)
    scaled = (pert_wide * jnp.sqrt(weight)).astype(jnp.bfloat16)
    identity = jnp.eye(members, dtype=jnp.float32)
    system = lax.dot_general(scaled, scaled, (((1,), (1,)), ((), ())), preferred_element_type=jnp.float32)
    system = system + (members - 1) / 1.1 * identity
    scaling = jnp.sqrt(jnp.sum(system * system))
    iterate = system / scaling
    inverse_root = identity
    for iteration in range(SWEEPS):
        middle = 1.5 * identity - 0.5 * jnp.dot(inverse_root, iterate, precision=exact_precision)
        iterate = jnp.dot(iterate, middle, precision=exact_precision)
        inverse_root = jnp.dot(middle, inverse_root, precision=exact_precision)
    forcing = jnp.dot(pert_wide, weight * innovation, precision=exact_precision)
    inner = jnp.dot(inverse_root, forcing, precision=exact_precision)
    mean_weight = jnp.dot(inverse_root, inner, precision=exact_precision) / scaling
    weights = (jnp.sqrt((members - 1) / scaling) * inverse_root + mean_weight[:, None]).astype(jnp.bfloat16)
    field_mean = lax.optimization_barrier(jnp.mean(fields, axis=0, dtype=jnp.float32))
    field_pert = (fields - field_mean).astype(jnp.bfloat16)
    updated = lax.dot_general(weights, field_pert, (((0,), (0,)), ((), ())), preferred_element_type=jnp.float32)
    return (updated + field_mean).astype(jnp.bfloat16)

def reference(ensemble, observations, precision, valid_count, position, level_kernel, listed_blocks):
    members = ensemble.shape[0]
    patches = PATCH_ROWS * PATCH_COLS
    zero = jnp.zeros((), jnp.int32)

    def patch_fields(number):
        grid_row = number // PATCH_COLS
        grid_col = number % PATCH_COLS
        block = lax.dynamic_index_in_dim(ensemble, grid_row, 1, keepdims=False)
        block = lax.dynamic_index_in_dim(block, grid_col, 1, keepdims=False)
        return block
    flat_position = position.reshape(patches, OWN_BLOCKS * SLOTS)

    def observe(number):
        fields = patch_fields(number).reshape(members, LEVELS, VARIABLES * COLUMNS)
        where_flat = flat_position[number]
        picked = fields[:, :, where_flat].astype(jnp.float32)
        factor = level_kernel[:, where_flat // COLUMNS]
        return lax.optimization_barrier(jnp.sum(picked * factor[None], axis=1)).astype(jnp.bfloat16)
    numbers = jnp.arange(patches, dtype=jnp.int32)
    equivalent = lax.map(observe, numbers)
    equivalent = equivalent.reshape(PATCH_ROWS, PATCH_COLS, members, OWN_BLOCKS, SLOTS)
    padded_equiv = jnp.pad(equivalent, ((1, 1), (1, 1), (0, 0), (0, 0), (0, 0)))
    slot_index = lax.broadcasted_iota(jnp.int32, precision.shape, 3)
    precision_used = jnp.where(slot_index < valid_count[..., None], precision, 0.0)
    pairs_all = jnp.stack([observations, precision_used], axis=2)
    padded_pairs = jnp.pad(pairs_all, ((1, 1), (1, 1), (0, 0), (0, 0), (0, 0)))
    flat_listed = listed_blocks.reshape(patches, LISTED)

    def analyse(number):
        grid_row = number // PATCH_COLS
        grid_col = number % PATCH_COLS
        near = lax.dynamic_slice(padded_equiv, (grid_row, grid_col, zero, zero, zero), (3, 3, members, OWN_BLOCKS, SLOTS))
        near = near.transpose(2, 0, 1, 3, 4).reshape(members, 9 * OWN_BLOCKS, SLOTS)
        near_pairs = lax.dynamic_slice(padded_pairs, (grid_row, grid_col, zero, zero, zero), (3, 3, 2, OWN_BLOCKS, SLOTS))
        near_pairs = near_pairs.transpose(2, 0, 1, 3, 4).reshape(2, 9 * OWN_BLOCKS, SLOTS)
        fields = patch_fields(number).reshape(members, LEVELS * VARIABLES * COLUMNS)
        return analyse_patch(near, near_pairs, flat_listed[number], fields)
    result = lax.map(analyse, numbers)
    result = result.reshape(PATCH_ROWS, PATCH_COLS, members, LEVELS, VARIABLES, COLUMNS)
    return result.transpose(2, 0, 1, 3, 4, 5)
```

```python
import functools

import jax
import jax.numpy as jnp
from jax import lax
from jax.experimental import pallas as pl
from jax.experimental.pallas import tpu as pltpu
from jax.sharding import PartitionSpec as P

VARIABLES = 12
COLUMNS = 1024
SLOTS = 128
OWN_BLOCKS = 2
LISTED = 8
SWEEPS = 6

MESH = pl.DeviceIdType.MESH
exact_precision = lax.Precision.HIGHEST


def observe(shaped_fields, where_flat, kernel):
    patch_count = where_flat.shape[0]
    slot_count = where_flat.shape[1]
    column_of = where_flat % COLUMNS
    variable_of = where_flat // COLUMNS
    column_iota = lax.broadcasted_iota(jnp.int32, (patch_count, COLUMNS, slot_count), 1)
    column_hot = (column_of[:, None, :] == column_iota).astype(jnp.bfloat16)
    spread = jnp.einsum(
        "kpvq,pqo->kpvo", shaped_fields, column_hot, preferred_element_type=jnp.float32
    )
    variable_iota = lax.broadcasted_iota(jnp.int32, (patch_count, VARIABLES, slot_count), 1)
    variable_weight = jnp.where(
        variable_of[:, None, :] == variable_iota, kernel[None, :, None], 0.0
    )
    return jnp.sum(spread * variable_weight[None], axis=2)


def wait_bytes(ref, sem):
    pltpu.make_async_copy(ref, ref, sem).wait()


def kernel(
    n,
    rows,
    listed_ref,
    fields_ref,
    equiv_ref,
    pairs_ref,
    out_ref,
    recv,
    done,
    near,
    near_pairs,
    scaled_ref,
    weights_ref,
    recv_sem,
    send_sem,
    back_sem,
    back_send_sem,
    near_sem,
    near_send_sem,
    pair_sem,
    pair_send_sem,
):
    me = lax.axis_index("member")
    row = lax.axis_index("patch")
    level = lax.axis_index("level")
    members = recv.shape[1] * recv.shape[2]

    def row_inside(step):
        return (row + step >= 0) & (row + step < rows)

    barrier = pltpu.get_barrier_semaphore()
    for step in (-1, 0, 1):

        @pl.when(row_inside(step))
        def _():
            def greet(other, carry):
                @pl.when((other != me) if step == 0 else (other >= 0))
                def _():
                    pl.semaphore_signal(
                        barrier, inc=1, device_id=(other, row + step, level), device_id_type=MESH
                    )

                return carry

            lax.fori_loop(0, n, greet, 0)

    row_count = 1 + jnp.where(row > 0, 1, 0) + jnp.where(row < rows - 1, 1, 0)
    pl.semaphore_wait(barrier, row_count * n - 1)

    for step in (-1, 0, 1):
        slot = 1 - step

        @pl.when(row_inside(step))
        def _():
            def send(shift, carry):
                other = lax.rem(me + shift, n)
                pltpu.make_async_remote_copy(
                    src_ref=equiv_ref.at[pl.ds(other, 3)],
                    dst_ref=near.at[slot, me],
                    send_sem=near_send_sem.at[slot],
                    recv_sem=near_sem.at[slot],
                    device_id=(other, row + step, level),
                    device_id_type=MESH,
                ).start()
                return carry

            lax.fori_loop(1 if step == 0 else 0, n, send, 0)

        @pl.when(jnp.logical_not(row_inside(step)))
        def _():
            near[1 + step] = jnp.zeros(near.shape[1:], near.dtype)

    pltpu.make_async_copy(equiv_ref.at[pl.ds(me, 3)], near.at[1, me], near_sem.at[1]).start()

    def pair_copy(step, shift):
        return pltpu.make_async_remote_copy(
            src_ref=pairs_ref,
            dst_ref=near_pairs.at[1 - step, 1 - shift],
            send_sem=pair_send_sem.at[1 - step, 1 - shift],
            recv_sem=pair_sem.at[1 - step, 1 - shift],
            device_id=(me + shift, row + step, level),
            device_id_type=MESH,
        )

    def pair_inside(step, shift):
        return row_inside(step) & (me + shift >= 0) & (me + shift < n)

    ring = [(a, b) for a in (-1, 0, 1) for b in (-1, 0, 1) if (a, b) != (0, 0)]
    for step, shift in ring:

        @pl.when(pair_inside(step, shift))
        def _():
            pair_copy(step, shift).start()

        @pl.when(jnp.logical_not(pair_inside(step, shift)))
        def _():
            near_pairs[1 + step, 1 + shift] = jnp.zeros(near_pairs.shape[2:], near_pairs.dtype)

    near_pairs[1, 1] = pairs_ref[...]

    def send_fields(v, carry):
        pltpu.make_async_copy(fields_ref.at[v, me], recv.at[v, me], recv_sem.at[v]).start()

        def send(shift, inner):
            other = lax.rem(me + shift, n)
            pltpu.make_async_remote_copy(
                src_ref=fields_ref.at[v, other],
                dst_ref=recv.at[v, me],
                send_sem=send_sem.at[v],
                recv_sem=recv_sem.at[v],
                device_id=(other, row, level),
                device_id_type=MESH,
            ).start()
            return inner

        return lax.fori_loop(1, n, send, carry)

    lax.fori_loop(0, VARIABLES, send_fields, 0)

    for step in (-1, 0, 1):

        @pl.when(row_inside(step))
        def _():
            wait_bytes(near.at[1 + step], near_sem.at[1 + step])

    for step, shift in ring:

        @pl.when(pair_inside(step, shift))
        def _():
            wait_bytes(near_pairs.at[1 + step, 1 + shift], pair_sem.at[1 + step, 1 + shift])

    def gather(entry, forcing):
        candidate = listed_ref[entry]
        place = candidate // OWN_BLOCKS
        block = candidate % OWN_BLOCKS
        down = place // 3
        across = place % 3
        moved = jnp.abs(down - 1) + jnp.abs(across - 1)
        taper = jnp.where(moved == 0, 1.0, jnp.where(moved == 1, 0.6, 0.35)).astype(jnp.float32)
        chosen = near[down, :, across, block].astype(jnp.float32).reshape(members, SLOTS)
        pairs = near_pairs[down, across]
        seen = jnp.where(block == 0, pairs[0:1], pairs[1:2])
        weight = jnp.where(block == 0, pairs[2:3], pairs[3:4]) * taper
        centre = jnp.sum(chosen, axis=0, keepdims=True) * (1.0 / members)
        pert = (chosen - centre).astype(jnp.bfloat16).astype(jnp.float32)
        scaled_ref[entry] = (pert * jnp.sqrt(weight)).astype(jnp.bfloat16)
        return forcing + jnp.sum(pert * (weight * (seen - centre)), axis=1, keepdims=True)

    forcing = lax.fori_loop(0, LISTED, gather, jnp.zeros((members, 1), jnp.float32))
    same = lax.broadcasted_iota(jnp.int32, (members, members), 0) == lax.broadcasted_iota(
        jnp.int32, (members, members), 1
    )
    identity = jnp.where(same, 1.0, 0.0).astype(jnp.float32)

    def outer(entry, system):
        part = scaled_ref[entry]
        return system + lax.dot_general(
            part, part, (((1,), (1,)), ((), ())), preferred_element_type=jnp.float32
        )

    system = lax.fori_loop(0, LISTED, outer, (members - 1) / 1.1 * identity)
    square = jnp.sum(jnp.sum(system * system, axis=1, keepdims=True), axis=0, keepdims=True)
    scaling = jnp.sqrt(square)

    def exact(a, b):
        return jnp.dot(a, b, precision=exact_precision, preferred_element_type=jnp.float32)

    def sweep(_, carry):
        iterate, inverse_root = carry
        middle = 1.5 * identity - 0.5 * exact(inverse_root, iterate)
        return exact(iterate, middle), exact(middle, inverse_root)

    _, inverse_root = lax.fori_loop(0, SWEEPS, sweep, (system / scaling, identity))
    wide = jnp.broadcast_to(forcing, (members, SLOTS))
    mean_weight = exact(inverse_root, exact(inverse_root, wide))[:, 0:1] / scaling
    weights = jnp.sqrt((members - 1) / scaling) * inverse_root + mean_weight
    weights_ref[...] = weights.T.astype(jnp.bfloat16)

    def apply(v, carry):
        wait_bytes(recv.at[v], recv_sem.at[v])
        fields = recv[v].astype(jnp.float32).reshape(members, COLUMNS)
        mean = jnp.sum(fields, axis=0, keepdims=True) * (1.0 / members)
        pert = (fields - mean).astype(jnp.bfloat16)
        updated = jnp.dot(weights_ref[...], pert, preferred_element_type=jnp.float32) + mean
        done[v] = updated.reshape(done.shape[1:]).astype(done.dtype)

        def send(shift, inner):
            other = lax.rem(me + shift, n)
            pltpu.make_async_remote_copy(
                src_ref=done.at[v, other],
                dst_ref=out_ref.at[v, me],
                send_sem=back_send_sem.at[v],
                recv_sem=back_sem.at[v],
                device_id=(other, row, level),
                device_id_type=MESH,
            ).start()
            return inner

        lax.fori_loop(1, n, send, 0)
        pltpu.make_async_copy(done.at[v, me], out_ref.at[v, me], back_sem.at[v]).start()
        return carry

    lax.fori_loop(0, VARIABLES, apply, 0)

    for step in (-1, 0, 1):

        @pl.when(row_inside(step))
        def _():
            count = n - 1 if step == 0 else n
            wait_bytes(near.at[1 - step, pl.ds(0, count)], near_send_sem.at[1 - step])

    for step, shift in ring:

        @pl.when(pair_inside(step, shift))
        def _():
            pair_copy(step, shift).wait_send()

    def finish(v, carry):
        wait_bytes(recv.at[v, pl.ds(0, n - 1)], send_sem.at[v])
        wait_bytes(done.at[v, pl.ds(0, n - 1)], back_send_sem.at[v])
        wait_bytes(done.at[v], back_sem.at[v])
        return carry

    lax.fori_loop(0, VARIABLES, finish, 0)


def body(ensemble, observations, precision, valid_count, position, level_kernel, listed_blocks):
    n = lax.axis_size("member")
    rows = lax.axis_size("patch")
    local_members = ensemble.shape[0]
    row_patches = ensemble.shape[2]
    members = local_members * n
    where_all = lax.all_gather(position, "member", axis=1, tiled=True)
    shaped_fields = ensemble.reshape(local_members, row_patches, VARIABLES, COLUMNS)
    level_term = observe(
        shaped_fields, where_all.reshape(row_patches, OWN_BLOCKS * SLOTS), level_kernel[0]
    )
    summed = lax.psum(level_term, "level")
    equiv = summed.astype(jnp.bfloat16).reshape(local_members, row_patches, OWN_BLOCKS, SLOTS)
    equiv = jnp.pad(equiv.transpose(1, 2, 0, 3), ((1, 1), (0, 0), (0, 0), (0, 0)))
    slot_index = lax.broadcasted_iota(jnp.int32, precision.shape, 3)
    precision_used = jnp.where(slot_index < valid_count[..., None], precision, 0.0)
    pairs = jnp.concatenate(
        [observations[0, 0], precision_used[0, 0], jnp.zeros((4, SLOTS), jnp.float32)]
    )
    fields = shaped_fields.transpose(2, 1, 0, 3)
    parts = (VARIABLES, n, local_members, COLUMNS)
    sem = pltpu.SemaphoreType.DMA
    result = pl.pallas_call(
        functools.partial(kernel, n, rows),
        out_shape=jax.ShapeDtypeStruct(parts, jnp.bfloat16),
        in_specs=[
            pl.BlockSpec(memory_space=pltpu.SMEM),
            pl.BlockSpec(memory_space=pl.ANY),
            pl.BlockSpec(memory_space=pltpu.VMEM),
            pl.BlockSpec(memory_space=pltpu.VMEM),
        ],
        out_specs=pl.BlockSpec(memory_space=pl.ANY),
        scratch_shapes=[
            pltpu.VMEM(parts, jnp.bfloat16),
            pltpu.VMEM(parts, jnp.bfloat16),
            pltpu.VMEM((3, n, 3, OWN_BLOCKS, local_members, SLOTS), jnp.bfloat16),
            pltpu.VMEM((3, 3, 8, SLOTS), jnp.float32),
            pltpu.VMEM((LISTED, members, SLOTS), jnp.bfloat16),
            pltpu.VMEM((members, members), jnp.bfloat16),
            sem((VARIABLES,)),
            sem((VARIABLES,)),
            sem((VARIABLES,)),
            sem((VARIABLES,)),
            sem((3,)),
            sem((3,)),
            sem((3, 3)),
            sem((3, 3)),
        ],
        compiler_params=pltpu.CompilerParams(
            collective_id=0, has_side_effects=True, vmem_limit_bytes=48 * 1024 * 1024
        ),
    )(listed_blocks[0, 0], fields, equiv, pairs)
    return result.transpose(2, 1, 0, 3).reshape(ensemble.shape)


def solution(mesh):
    placed = (
        P("member", "patch", None, "level", None, None),
        P("patch", "member", None, None),
        P("patch", "member", None, None),
        P("patch", "member", None),
        P("patch", "member", None, None),
        P("level", None),
        P("patch", "member", None),
    )
    return jax.shard_map(
        body,
        mesh=mesh,
        in_specs=placed,
        out_specs=P("member", "patch", None, "level", None, None),
        check_vma=False,
    )
```

```python
import functools

import jax
import jax.numpy as jnp
from jax import lax
from jax.experimental import pallas as pl
from jax.experimental.pallas import tpu as pltpu
from jax.sharding import PartitionSpec as P

VARIABLES = 12
COLUMNS = 1024
SLOTS = 128
OWN_BLOCKS = 2
LISTED = 8
SWEEPS = 6

MESH = pl.DeviceIdType.MESH
exact_precision = lax.Precision.HIGHEST


def wait_bytes(ref, sem):
    pltpu.make_async_copy(ref, ref, sem).wait()


def kernel(
    n,
    rows,
    lead,
    listed_ref,
    valid_ref,
    level_ref,
    ensemble_ref,
    position_ref,
    observed_ref,
    precision_ref,
    out_ref,
    loaded,
    fields_ref,
    recv,
    done,
    where_ref,
    term_ref,
    other_term,
    equiv_ref,
    near,
    pairs_ref,
    near_pairs,
    scaled_ref,
    weights_ref,
    load_sem,
    recv_sem,
    send_sem,
    back_sem,
    back_send_sem,
    where_sem,
    term_sem,
    own_sem,
    row_sem,
    core_sem,
    pair_sem,
    pair_send_sem,
):
    me = lax.axis_index("member")
    row = lax.axis_index("patch")
    level = lax.axis_index("level")
    local_members = recv.shape[2]
    members = n * local_members
    sibling = (me, row, 1 - level)

    def row_inside(step):
        return (row + step >= 0) & (row + step < rows)

    def load(v, carry):
        pltpu.make_async_copy(ensemble_ref.at[:, v], loaded.at[v], load_sem.at[v]).start()
        return carry

    lax.fori_loop(0, VARIABLES, load, 0)

    barrier = pltpu.get_barrier_semaphore()
    for step in (-1, 0, 1):

        @pl.when(row_inside(step))
        def _():
            def greet(other, carry):
                @pl.when((other != me) if step == 0 else (other >= 0))
                def _():
                    pl.semaphore_signal(
                        barrier, inc=1, device_id=(other, row + step, level), device_id_type=MESH
                    )

                return carry

            lax.fori_loop(0, n, greet, 0)

    pl.semaphore_signal(barrier, inc=1, device_id=sibling, device_id_type=MESH)
    row_count = 1 + jnp.where(row > 0, 1, 0) + jnp.where(row < rows - 1, 1, 0)
    pl.semaphore_wait(barrier, row_count * n)

    where_ref[me] = jnp.zeros(where_ref.shape[1:], where_ref.dtype)
    where_ref[me, 0:OWN_BLOCKS] = position_ref[...]

    def send_where(shift, carry):
        pltpu.make_async_remote_copy(
            src_ref=where_ref.at[me],
            dst_ref=where_ref.at[me],
            send_sem=where_sem.at[0],
            recv_sem=where_sem.at[1],
            device_id=(lax.rem(me + shift, n), row, level),
            device_id_type=MESH,
        ).start()
        return carry

    lax.fori_loop(1, n, send_where, 0)

    slot_index = lax.broadcasted_iota(jnp.int32, (1, SLOTS), 1)
    pairs_ref[...] = jnp.zeros(pairs_ref.shape, pairs_ref.dtype)
    for block in range(OWN_BLOCKS):
        pairs_ref[block] = observed_ref[block]
        kept = jnp.where(slot_index < valid_ref[block], precision_ref[block : block + 1], 0.0)
        pairs_ref[OWN_BLOCKS + block : OWN_BLOCKS + block + 1] = kept

    def pair_copy(step, shift):
        return pltpu.make_async_remote_copy(
            src_ref=pairs_ref,
            dst_ref=near_pairs.at[1 - step, 1 - shift],
            send_sem=pair_send_sem.at[1 - step, 1 - shift],
            recv_sem=pair_sem.at[1 - step, 1 - shift],
            device_id=(me + shift, row + step, level),
            device_id_type=MESH,
        )

    def pair_inside(step, shift):
        return row_inside(step) & (me + shift >= 0) & (me + shift < n)

    ring = [(a, b) for a in (-1, 0, 1) for b in (-1, 0, 1) if (a, b) != (0, 0)]
    for step, shift in ring:

        @pl.when(pair_inside(step, shift))
        def _():
            pair_copy(step, shift).start()

        @pl.when(jnp.logical_not(pair_inside(step, shift)))
        def _():
            near_pairs[1 + step, 1 + shift] = jnp.zeros(near_pairs.shape[2:], near_pairs.dtype)

    near_pairs[1, 1] = pairs_ref[...]

    def arrange(v, carry):
        wait_bytes(loaded.at[v], load_sem.at[v])
        turned = jnp.transpose(loaded[v].astype(jnp.float32), (1, 0, 2))
        fields_ref[v] = turned.astype(jnp.bfloat16)
        return carry

    def send_fields(v, carry):
        def send(shift, inner):
            other = lax.rem(me + shift, n)
            pltpu.make_async_remote_copy(
                src_ref=fields_ref.at[v, other],
                dst_ref=recv.at[v, me],
                send_sem=send_sem.at[v],
                recv_sem=recv_sem.at[v],
                device_id=(other, row, level),
                device_id_type=MESH,
            ).start()
            return inner

        lax.fori_loop(1, n, send, 0)
        pltpu.make_async_copy(fields_ref.at[v, me], recv.at[v, me], recv_sem.at[v]).start()
        return carry

    def arrange_and_send(v, carry):
        return send_fields(v, arrange(v, carry))

    lax.fori_loop(0, lead, arrange_and_send, 0)
    lax.fori_loop(lead, VARIABLES, arrange, 0)

    wait_bytes(where_ref.at[pl.ds(0, n - 1)], where_sem.at[1])
    column_iota = lax.broadcasted_iota(jnp.int32, (COLUMNS, OWN_BLOCKS * SLOTS), 0)

    def observe(p, carry):
        where = where_ref[p]
        where = jnp.concatenate([where[b : b + 1] for b in range(OWN_BLOCKS)], axis=1)
        variable_of = where // COLUMNS
        hot = jnp.where(where - variable_of * COLUMNS == column_iota, 1.0, 0.0)
        fields = fields_ref[:, p]
        if local_members % 16:
            fields = fields.astype(jnp.float32)
        fields = fields.reshape(VARIABLES * local_members, COLUMNS).astype(jnp.bfloat16)
        spread = jnp.dot(fields, hot.astype(jnp.bfloat16), preferred_element_type=jnp.float32)
        total = jnp.zeros((local_members, OWN_BLOCKS * SLOTS), jnp.float32)
        for v in range(VARIABLES):
            factor = jnp.where(variable_of == v, level_ref[v], 0.0)
            total = total + spread[v * local_members : (v + 1) * local_members] * factor
        for b in range(OWN_BLOCKS):
            term_ref[b, p] = total[:, b * SLOTS : (b + 1) * SLOTS]
        return carry

    lax.fori_loop(0, n, observe, 0)
    term_copy = pltpu.make_async_remote_copy(
        src_ref=term_ref.at[1 - level],
        dst_ref=other_term,
        send_sem=term_sem.at[0],
        recv_sem=term_sem.at[1],
        device_id=sibling,
        device_id_type=MESH,
    )
    term_copy.start()
    lax.fori_loop(lead, lead + 1, send_fields, 0)
    term_copy.wait_recv()
    equiv_ref[0] = jnp.zeros(equiv_ref.shape[1:], equiv_ref.dtype)
    equiv_ref[n + 1] = jnp.zeros(equiv_ref.shape[1:], equiv_ref.dtype)

    def add_levels(p, carry):
        equiv_ref[p + 1] = (term_ref[level, p] + other_term[p]).astype(jnp.bfloat16)
        return carry

    lax.fori_loop(0, n, add_levels, 0)

    def send_own(shift, carry):
        other = lax.rem(me + shift, n)
        pltpu.make_async_remote_copy(
            src_ref=equiv_ref.at[pl.ds(other, 3)],
            dst_ref=near.at[level, 1, me],
            send_sem=own_sem.at[0],
            recv_sem=own_sem.at[1],
            device_id=(other, row, level),
            device_id_type=MESH,
        ).start()
        return carry

    lax.fori_loop(1, n, send_own, 0)
    pltpu.make_async_copy(
        equiv_ref.at[pl.ds(me, 3)], near.at[level, 1, me], own_sem.at[1]
    ).start()
    lax.fori_loop(lead + 1, lead + 2, send_fields, 0)
    wait_bytes(near.at[level, 1], own_sem.at[1])

    def row_copy(step):
        return pltpu.make_async_remote_copy(
            src_ref=near.at[level, 1],
            dst_ref=near.at[level, 1 - step],
            send_sem=row_sem.at[0, 1 - step],
            recv_sem=row_sem.at[1, 1 - step],
            device_id=(me, row + step, level),
            device_id_type=MESH,
        )

    for step in (-1, 1):

        @pl.when(row_inside(step))
        def _():
            row_copy(step).start()

        @pl.when(jnp.logical_not(row_inside(step)))
        def _():
            near[level, 1 + step] = jnp.zeros(near.shape[2:], near.dtype)

    lax.fori_loop(lead + 2, lead + 3, send_fields, 0)
    for step in (-1, 1):

        @pl.when(row_inside(step))
        def _():
            wait_bytes(near.at[level, 1 + step], row_sem.at[1, 1 + step])

    core_copy = pltpu.make_async_remote_copy(
        src_ref=near.at[level],
        dst_ref=near.at[level],
        send_sem=core_sem.at[0],
        recv_sem=core_sem.at[1],
        device_id=sibling,
        device_id_type=MESH,
    )
    core_copy.start()
    lax.fori_loop(lead + 3, VARIABLES, send_fields, 0)
    wait_bytes(near.at[1 - level], core_sem.at[1])

    for step, shift in ring:

        @pl.when(pair_inside(step, shift))
        def _():
            wait_bytes(near_pairs.at[1 + step, 1 + shift], pair_sem.at[1 + step, 1 + shift])

    def gather(entry, forcing):
        candidate = listed_ref[entry]
        place = candidate // OWN_BLOCKS
        block = candidate % OWN_BLOCKS
        down = place // 3
        across = place % 3
        moved = jnp.abs(down - 1) + jnp.abs(across - 1)
        taper = jnp.where(moved == 0, 1.0, jnp.where(moved == 1, 0.6, 0.35)).astype(jnp.float32)
        chosen = near[block, down, :, across].astype(jnp.float32).reshape(members, SLOTS)
        pairs = near_pairs[down, across]
        seen = jnp.where(block == 0, pairs[0:1], pairs[1:2])
        weight = jnp.where(block == 0, pairs[2:3], pairs[3:4]) * taper
        centre = jnp.sum(chosen, axis=0, keepdims=True) * (1.0 / members)
        pert = (chosen - centre).astype(jnp.bfloat16).astype(jnp.float32)
        scaled_ref[entry] = (pert * jnp.sqrt(weight)).astype(jnp.bfloat16)
        return forcing + jnp.sum(pert * (weight * (seen - centre)), axis=1, keepdims=True)

    forcing = lax.fori_loop(0, LISTED, gather, jnp.zeros((members, 1), jnp.float32))
    same = lax.broadcasted_iota(jnp.int32, (members, members), 0) == lax.broadcasted_iota(
        jnp.int32, (members, members), 1
    )
    identity = jnp.where(same, 1.0, 0.0).astype(jnp.float32)

    def outer(entry, system):
        part = scaled_ref[entry]
        return system + lax.dot_general(
            part, part, (((1,), (1,)), ((), ())), preferred_element_type=jnp.float32
        )

    system = lax.fori_loop(0, LISTED, outer, (members - 1) / 1.1 * identity)
    square = jnp.sum(jnp.sum(system * system, axis=1, keepdims=True), axis=0, keepdims=True)
    scaling = jnp.sqrt(square)

    def exact(a, b):
        return jnp.dot(a, b, precision=exact_precision, preferred_element_type=jnp.float32)

    def sweep(_, carry):
        iterate, inverse_root = carry
        middle = 1.5 * identity - 0.5 * exact(inverse_root, iterate)
        return exact(iterate, middle), exact(middle, inverse_root)

    _, inverse_root = lax.fori_loop(0, SWEEPS, sweep, (system / scaling, identity))
    wide = jnp.broadcast_to(forcing, (members, SLOTS))
    mean_weight = exact(inverse_root, exact(inverse_root, wide))[:, 0:1] / scaling
    weights = jnp.sqrt((members - 1) / scaling) * inverse_root + mean_weight
    weights_ref[...] = weights.T.astype(jnp.bfloat16)

    def apply(v, carry):
        wait_bytes(recv.at[v], recv_sem.at[v])
        fields = recv[v].astype(jnp.float32).reshape(members, COLUMNS)
        mean = jnp.sum(fields, axis=0, keepdims=True) * (1.0 / members)
        pert = (fields - mean).astype(jnp.bfloat16)
        updated = jnp.dot(weights_ref[...], pert, preferred_element_type=jnp.float32) + mean
        done[v] = updated.reshape(done.shape[1:]).astype(done.dtype)

        def send(shift, inner):
            other = lax.rem(me + shift, n)
            pltpu.make_async_remote_copy(
                src_ref=done.at[v, other],
                dst_ref=out_ref.at[v, me],
                send_sem=back_send_sem.at[v],
                recv_sem=back_sem.at[v],
                device_id=(other, row, level),
                device_id_type=MESH,
            ).start()
            return inner

        lax.fori_loop(1, n, send, 0)
        pltpu.make_async_copy(done.at[v, me], out_ref.at[v, me], back_sem.at[v]).start()
        return carry

    lax.fori_loop(0, VARIABLES, apply, 0)

    wait_bytes(where_ref.at[pl.ds(0, n - 1)], where_sem.at[0])
    term_copy.wait_send()
    wait_bytes(near.at[0, 1, pl.ds(0, n - 1)], own_sem.at[0])
    for step in (-1, 1):

        @pl.when(row_inside(step))
        def _():
            row_copy(step).wait_send()

    core_copy.wait_send()
    for step, shift in ring:

        @pl.when(pair_inside(step, shift))
        def _():
            pair_copy(step, shift).wait_send()

    def finish(v, carry):
        wait_bytes(recv.at[v, pl.ds(0, n - 1)], send_sem.at[v])
        wait_bytes(done.at[v, pl.ds(0, n - 1)], back_send_sem.at[v])
        wait_bytes(done.at[v], back_sem.at[v])
        return carry

    lax.fori_loop(0, VARIABLES, finish, 0)


def body(ensemble, observations, precision, valid_count, position, level_kernel, listed_blocks):
    n = lax.axis_size("member")
    rows = lax.axis_size("patch")
    local_members = ensemble.shape[0]
    members = local_members * n
    lead = 4
    shaped = ensemble.reshape(local_members, n, VARIABLES, COLUMNS).transpose(0, 2, 1, 3)
    parts = (VARIABLES, n, local_members, COLUMNS)
    sem = pltpu.SemaphoreType.DMA
    smem = pl.BlockSpec(memory_space=pltpu.SMEM)
    vmem = pl.BlockSpec(memory_space=pltpu.VMEM)
    whole = pl.BlockSpec(memory_space=pl.ANY)
    result = pl.pallas_call(
        functools.partial(kernel, n, rows, lead),
        out_shape=jax.ShapeDtypeStruct(parts, jnp.bfloat16),
        in_specs=[smem, smem, smem, whole, vmem, vmem, vmem],
        out_specs=whole,
        scratch_shapes=[
            pltpu.VMEM((VARIABLES, local_members, n, COLUMNS), jnp.bfloat16),
            pltpu.VMEM(parts, jnp.bfloat16),
            pltpu.VMEM(parts, jnp.bfloat16),
            pltpu.VMEM(parts, jnp.bfloat16),
            pltpu.VMEM((n, 8, SLOTS), jnp.int32),
            pltpu.VMEM((OWN_BLOCKS, n, local_members, SLOTS), jnp.float32),
            pltpu.VMEM((n, local_members, SLOTS), jnp.float32),
            pltpu.VMEM((n + 2, local_members, SLOTS), jnp.bfloat16),
            pltpu.VMEM((OWN_BLOCKS, 3, n, 3, local_members, SLOTS), jnp.bfloat16),
            pltpu.VMEM((8, SLOTS), jnp.float32),
            pltpu.VMEM((3, 3, 8, SLOTS), jnp.float32),
            pltpu.VMEM((LISTED, members, SLOTS), jnp.bfloat16),
            pltpu.VMEM((members, members), jnp.bfloat16),
            sem((VARIABLES,)),
            sem((VARIABLES,)),
            sem((VARIABLES,)),
            sem((VARIABLES,)),
            sem((VARIABLES,)),
            sem((2,)),
            sem((2,)),
            sem((2,)),
            sem((2, 3)),
            sem((2,)),
            sem((3, 3)),
            sem((3, 3)),
        ],
        compiler_params=pltpu.CompilerParams(
            collective_id=0, has_side_effects=True, vmem_limit_bytes=56 * 1024 * 1024
        ),
    )(
        listed_blocks[0, 0],
        valid_count[0, 0],
        level_kernel[0],
        shaped,
        position[0, 0],
        observations[0, 0],
        precision[0, 0],
    )
    return result.transpose(2, 1, 0, 3).reshape(ensemble.shape)


def solution(mesh):
    placed = (
        P("member", "patch", None, "level", None, None),
        P("patch", "member", None, None),
        P("patch", "member", None, None),
        P("patch", "member", None),
        P("patch", "member", None, None),
        P("level", None),
        P("patch", "member", None),
    )
    return jax.shard_map(
        body,
        mesh=mesh,
        in_specs=placed,
        out_specs=P("member", "patch", None, "level", None, None),
        check_vma=False,
    )
```

```python
import functools

import jax
import jax.numpy as jnp
from jax import lax
from jax.experimental import pallas as pl
from jax.experimental.pallas import tpu as pltpu
from jax.sharding import PartitionSpec as P

VARIABLES = 12
COLUMNS = 1024
SLOTS = 128
OWN_BLOCKS = 2
LISTED = 8
SWEEPS = 6

MESH = pl.DeviceIdType.MESH
exact_precision = lax.Precision.HIGHEST


def wait_bytes(ref, sem):
    pltpu.make_async_copy(ref, ref, sem).wait()


def kernel(
    n,
    rows,
    lead,
    listed_ref,
    valid_ref,
    level_ref,
    ensemble_ref,
    position_ref,
    observed_ref,
    precision_ref,
    out_ref,
    landed,
    loaded,
    fields_ref,
    recv,
    done,
    where_ref,
    term_ref,
    other_term,
    equiv_ref,
    near,
    pairs_ref,
    near_pairs,
    scaled_ref,
    weights_ref,
    load_sem,
    recv_sem,
    send_sem,
    back_sem,
    back_send_sem,
    where_sem,
    term_sem,
    own_sem,
    row_sem,
    core_sem,
    pair_sem,
    pair_send_sem,
):
    me = lax.axis_index("member")
    row = lax.axis_index("patch")
    level = lax.axis_index("level")
    local_members = recv.shape[2]
    members = n * local_members
    sibling = (me, row, 1 - level)

    def row_inside(step):
        return (row + step >= 0) & (row + step < rows)

    def load(v, carry):
        pltpu.make_async_copy(ensemble_ref.at[:, v], loaded.at[v], load_sem.at[v]).start()
        return carry

    lax.fori_loop(0, VARIABLES, load, 0)

    barrier = pltpu.get_barrier_semaphore()
    for step in (-1, 0, 1):

        @pl.when(row_inside(step))
        def _():
            def greet(other, carry):
                @pl.when((other != me) if step == 0 else (other >= 0))
                def _():
                    pl.semaphore_signal(
                        barrier, inc=1, device_id=(other, row + step, level), device_id_type=MESH
                    )

                return carry

            lax.fori_loop(0, n, greet, 0)

    pl.semaphore_signal(barrier, inc=1, device_id=sibling, device_id_type=MESH)

    def arrange(v, carry):
        wait_bytes(loaded.at[v], load_sem.at[v])
        turned = jnp.transpose(loaded[v].astype(jnp.float32), (1, 0, 2))
        fields_ref[v] = turned.astype(jnp.bfloat16)
        return carry

    arrange(0, 0)
    row_count = 1 + jnp.where(row > 0, 1, 0) + jnp.where(row < rows - 1, 1, 0)
    pl.semaphore_wait(barrier, row_count * n)

    where_ref[me] = jnp.zeros(where_ref.shape[1:], where_ref.dtype)
    where_ref[me, 0:OWN_BLOCKS] = position_ref[...]

    def send_where(shift, carry):
        pltpu.make_async_remote_copy(
            src_ref=where_ref.at[me],
            dst_ref=where_ref.at[me],
            send_sem=where_sem.at[0],
            recv_sem=where_sem.at[1],
            device_id=(lax.rem(me + shift, n), row, level),
            device_id_type=MESH,
        ).start()
        return carry

    lax.fori_loop(1, n, send_where, 0)

    def send_fields(v, carry):
        def send(shift, inner):
            other = lax.rem(me + shift, n)
            pltpu.make_async_remote_copy(
                src_ref=fields_ref.at[v, other],
                dst_ref=recv.at[v, me],
                send_sem=send_sem.at[v],
                recv_sem=recv_sem.at[v],
                device_id=(other, row, level),
                device_id_type=MESH,
            ).start()
            return inner

        lax.fori_loop(1, n, send, 0)
        pltpu.make_async_copy(fields_ref.at[v, me], recv.at[v, me], recv_sem.at[v]).start()
        return carry

    send_fields(0, 0)

    slot_index = lax.broadcasted_iota(jnp.int32, (1, SLOTS), 1)
    pairs_ref[...] = jnp.zeros(pairs_ref.shape, pairs_ref.dtype)
    for block in range(OWN_BLOCKS):
        pairs_ref[block] = observed_ref[block]
        kept = jnp.where(slot_index < valid_ref[block], precision_ref[block : block + 1], 0.0)
        pairs_ref[OWN_BLOCKS + block : OWN_BLOCKS + block + 1] = kept

    def pair_copy(step, shift):
        return pltpu.make_async_remote_copy(
            src_ref=pairs_ref,
            dst_ref=near_pairs.at[1 - step, 1 - shift],
            send_sem=pair_send_sem.at[1 - step, 1 - shift],
            recv_sem=pair_sem.at[1 - step, 1 - shift],
            device_id=(me + shift, row + step, level),
            device_id_type=MESH,
        )

    def pair_inside(step, shift):
        return row_inside(step) & (me + shift >= 0) & (me + shift < n)

    ring = [(a, b) for a in (-1, 0, 1) for b in (-1, 0, 1) if (a, b) != (0, 0)]
    for step, shift in ring:

        @pl.when(pair_inside(step, shift))
        def _():
            pair_copy(step, shift).start()

        @pl.when(jnp.logical_not(pair_inside(step, shift)))
        def _():
            near_pairs[1 + step, 1 + shift] = jnp.zeros(near_pairs.shape[2:], near_pairs.dtype)

    near_pairs[1, 1] = pairs_ref[...]

    def arrange_and_send(v, carry):
        return send_fields(v, arrange(v, carry))

    lax.fori_loop(1, lead, arrange_and_send, 0)
    lax.fori_loop(lead, VARIABLES, arrange, 0)

    wait_bytes(where_ref.at[pl.ds(0, n - 1)], where_sem.at[1])
    column_iota = lax.broadcasted_iota(jnp.int32, (COLUMNS, OWN_BLOCKS * SLOTS), 0)

    def observe(p, carry):
        where = where_ref[p]
        where = jnp.concatenate([where[b : b + 1] for b in range(OWN_BLOCKS)], axis=1)
        variable_of = where // COLUMNS
        hot = jnp.where(where - variable_of * COLUMNS == column_iota, 1.0, 0.0)
        fields = fields_ref[:, p]
        if local_members % 16:
            fields = fields.astype(jnp.float32)
        fields = fields.reshape(VARIABLES * local_members, COLUMNS).astype(jnp.bfloat16)
        spread = jnp.dot(fields, hot.astype(jnp.bfloat16), preferred_element_type=jnp.float32)
        total = jnp.zeros((local_members, OWN_BLOCKS * SLOTS), jnp.float32)
        for v in range(VARIABLES):
            factor = jnp.where(variable_of == v, level_ref[v], 0.0)
            total = total + spread[v * local_members : (v + 1) * local_members] * factor
        for b in range(OWN_BLOCKS):
            term_ref[b, p] = total[:, b * SLOTS : (b + 1) * SLOTS]
        return carry

    lax.fori_loop(0, n, observe, 0)
    term_copy = pltpu.make_async_remote_copy(
        src_ref=term_ref.at[1 - level],
        dst_ref=other_term,
        send_sem=term_sem.at[0],
        recv_sem=term_sem.at[1],
        device_id=sibling,
        device_id_type=MESH,
    )
    term_copy.start()
    lax.fori_loop(lead, lead + 1, send_fields, 0)
    term_copy.wait_recv()
    equiv_ref[0] = jnp.zeros(equiv_ref.shape[1:], equiv_ref.dtype)
    equiv_ref[n + 1] = jnp.zeros(equiv_ref.shape[1:], equiv_ref.dtype)

    def add_levels(p, carry):
        equiv_ref[p + 1] = (term_ref[level, p] + other_term[p]).astype(jnp.bfloat16)
        return carry

    lax.fori_loop(0, n, add_levels, 0)

    def send_own(shift, carry):
        other = lax.rem(me + shift, n)
        pltpu.make_async_remote_copy(
            src_ref=equiv_ref.at[pl.ds(other, 3)],
            dst_ref=near.at[level, 1, me],
            send_sem=own_sem.at[0],
            recv_sem=own_sem.at[1],
            device_id=(other, row, level),
            device_id_type=MESH,
        ).start()
        return carry

    lax.fori_loop(1, n, send_own, 0)
    pltpu.make_async_copy(
        equiv_ref.at[pl.ds(me, 3)], near.at[level, 1, me], own_sem.at[1]
    ).start()
    lax.fori_loop(lead + 1, lead + 2, send_fields, 0)
    wait_bytes(near.at[level, 1], own_sem.at[1])

    def row_copy(step):
        return pltpu.make_async_remote_copy(
            src_ref=near.at[level, 1],
            dst_ref=near.at[level, 1 - step],
            send_sem=row_sem.at[0, 1 - step],
            recv_sem=row_sem.at[1, 1 - step],
            device_id=(me, row + step, level),
            device_id_type=MESH,
        )

    for step in (-1, 1):

        @pl.when(row_inside(step))
        def _():
            row_copy(step).start()

        @pl.when(jnp.logical_not(row_inside(step)))
        def _():
            near[level, 1 + step] = jnp.zeros(near.shape[2:], near.dtype)

    lax.fori_loop(lead + 2, lead + 3, send_fields, 0)
    for step in (-1, 1):

        @pl.when(row_inside(step))
        def _():
            wait_bytes(near.at[level, 1 + step], row_sem.at[1, 1 + step])

    core_copy = pltpu.make_async_remote_copy(
        src_ref=near.at[level],
        dst_ref=near.at[level],
        send_sem=core_sem.at[0],
        recv_sem=core_sem.at[1],
        device_id=sibling,
        device_id_type=MESH,
    )
    core_copy.start()
    lax.fori_loop(lead + 3, VARIABLES, send_fields, 0)
    wait_bytes(near.at[1 - level], core_sem.at[1])

    for step, shift in ring:

        @pl.when(pair_inside(step, shift))
        def _():
            wait_bytes(near_pairs.at[1 + step, 1 + shift], pair_sem.at[1 + step, 1 + shift])

    def gather(entry, forcing):
        candidate = listed_ref[entry]
        place = candidate // OWN_BLOCKS
        block = candidate % OWN_BLOCKS
        down = place // 3
        across = place % 3
        moved = jnp.abs(down - 1) + jnp.abs(across - 1)
        taper = jnp.where(moved == 0, 1.0, jnp.where(moved == 1, 0.6, 0.35)).astype(jnp.float32)
        chosen = near[block, down, :, across].astype(jnp.float32).reshape(members, SLOTS)
        pairs = near_pairs[down, across]
        seen = jnp.where(block == 0, pairs[0:1], pairs[1:2])
        weight = jnp.where(block == 0, pairs[2:3], pairs[3:4]) * taper
        centre = jnp.sum(chosen, axis=0, keepdims=True) * (1.0 / members)
        pert = (chosen - centre).astype(jnp.bfloat16).astype(jnp.float32)
        scaled_ref[entry] = (pert * jnp.sqrt(weight)).astype(jnp.bfloat16)
        return forcing + jnp.sum(pert * (weight * (seen - centre)), axis=1, keepdims=True)

    forcing = lax.fori_loop(0, LISTED, gather, jnp.zeros((members, 1), jnp.float32))
    same = lax.broadcasted_iota(jnp.int32, (members, members), 0) == lax.broadcasted_iota(
        jnp.int32, (members, members), 1
    )
    identity = jnp.where(same, 1.0, 0.0).astype(jnp.float32)

    def outer(entry, system):
        part = scaled_ref[entry]
        return system + lax.dot_general(
            part, part, (((1,), (1,)), ((), ())), preferred_element_type=jnp.float32
        )

    system = lax.fori_loop(0, LISTED, outer, (members - 1) / 1.1 * identity)
    square = jnp.sum(jnp.sum(system * system, axis=1, keepdims=True), axis=0, keepdims=True)
    scaling = jnp.sqrt(square)

    def exact(a, b):
        return jnp.dot(a, b, precision=exact_precision, preferred_element_type=jnp.float32)

    def sweep(_, carry):
        iterate, inverse_root = carry
        middle = 1.5 * identity - 0.5 * exact(inverse_root, iterate)
        return exact(iterate, middle), exact(middle, inverse_root)

    _, inverse_root = lax.fori_loop(0, SWEEPS, sweep, (system / scaling, identity))
    wide = jnp.broadcast_to(forcing, (members, SLOTS))
    mean_weight = exact(inverse_root, exact(inverse_root, wide))[:, 0:1] / scaling
    weights = jnp.sqrt((members - 1) / scaling) * inverse_root + mean_weight
    weights_ref[...] = weights.T.astype(jnp.bfloat16)

    def apply(v, carry):
        wait_bytes(recv.at[v], recv_sem.at[v])
        fields = recv[v].astype(jnp.float32).reshape(members, COLUMNS)
        mean = jnp.sum(fields, axis=0, keepdims=True) * (1.0 / members)
        pert = (fields - mean).astype(jnp.bfloat16)
        updated = jnp.dot(weights_ref[...], pert, preferred_element_type=jnp.float32) + mean
        done[v] = updated.reshape(done.shape[1:]).astype(done.dtype)

        def send(shift, inner):
            other = lax.rem(me + shift, n)
            pltpu.make_async_remote_copy(
                src_ref=done.at[v, other],
                dst_ref=landed.at[v, me],
                send_sem=back_send_sem.at[v],
                recv_sem=back_sem.at[v],
                device_id=(other, row, level),
                device_id_type=MESH,
            ).start()
            return inner

        lax.fori_loop(1, n, send, 0)
        pltpu.make_async_copy(done.at[v, me], landed.at[v, me], back_sem.at[v]).start()
        return carry

    lax.fori_loop(0, VARIABLES, apply, 0)

    def restore(v, carry):
        wait_bytes(landed.at[v], back_sem.at[v])
        turned = jnp.transpose(landed[v].astype(jnp.float32), (1, 0, 2))
        loaded[v] = turned.astype(jnp.bfloat16)
        pltpu.make_async_copy(loaded.at[v], out_ref.at[:, v], load_sem.at[v]).start()
        return carry


    lax.fori_loop(0, VARIABLES, restore, 0)
    wait_bytes(where_ref.at[pl.ds(0, n - 1)], where_sem.at[0])
    term_copy.wait_send()
    wait_bytes(near.at[0, 1, pl.ds(0, n - 1)], own_sem.at[0])
    for step in (-1, 1):

        @pl.when(row_inside(step))
        def _():
            row_copy(step).wait_send()

    core_copy.wait_send()
    for step, shift in ring:

        @pl.when(pair_inside(step, shift))
        def _():
            pair_copy(step, shift).wait_send()

    def finish(v, carry):
        wait_bytes(recv.at[v, pl.ds(0, n - 1)], send_sem.at[v])
        wait_bytes(done.at[v, pl.ds(0, n - 1)], back_send_sem.at[v])
        wait_bytes(loaded.at[v], load_sem.at[v])
        return carry

    lax.fori_loop(0, VARIABLES, finish, 0)


def body(ensemble, observations, precision, valid_count, position, level_kernel, listed_blocks):
    n = lax.axis_size("member")
    rows = lax.axis_size("patch")
    local_members = ensemble.shape[0]
    members = local_members * n
    lead = 4
    shaped = ensemble.reshape(local_members, n, VARIABLES, COLUMNS).transpose(0, 2, 1, 3)
    parts = (VARIABLES, n, local_members, COLUMNS)
    sem = pltpu.SemaphoreType.DMA
    smem = pl.BlockSpec(memory_space=pltpu.SMEM)
    vmem = pl.BlockSpec(memory_space=pltpu.VMEM)
    whole = pl.BlockSpec(memory_space=pl.ANY)
    result = pl.pallas_call(
        functools.partial(kernel, n, rows, lead),
        out_shape=jax.ShapeDtypeStruct(shaped.shape, jnp.bfloat16),
        in_specs=[smem, smem, smem, whole, vmem, vmem, vmem],
        out_specs=whole,
        scratch_shapes=[
            pltpu.VMEM(parts, jnp.bfloat16),
            pltpu.VMEM((VARIABLES, local_members, n, COLUMNS), jnp.bfloat16),
            pltpu.VMEM(parts, jnp.bfloat16),
            pltpu.VMEM(parts, jnp.bfloat16),
            pltpu.VMEM(parts, jnp.bfloat16),
            pltpu.VMEM((n, 8, SLOTS), jnp.int32),
            pltpu.VMEM((OWN_BLOCKS, n, local_members, SLOTS), jnp.float32),
            pltpu.VMEM((n, local_members, SLOTS), jnp.float32),
            pltpu.VMEM((n + 2, local_members, SLOTS), jnp.bfloat16),
            pltpu.VMEM((OWN_BLOCKS, 3, n, 3, local_members, SLOTS), jnp.bfloat16),
            pltpu.VMEM((8, SLOTS), jnp.float32),
            pltpu.VMEM((3, 3, 8, SLOTS), jnp.float32),
            pltpu.VMEM((LISTED, members, SLOTS), jnp.bfloat16),
            pltpu.VMEM((members, members), jnp.bfloat16),
            sem((VARIABLES,)),
            sem((VARIABLES,)),
            sem((VARIABLES,)),
            sem((VARIABLES,)),
            sem((VARIABLES,)),
            sem((2,)),
            sem((2,)),
            sem((2,)),
            sem((2, 3)),
            sem((2,)),
            sem((3, 3)),
            sem((3, 3)),
        ],
        compiler_params=pltpu.CompilerParams(
            collective_id=0, has_side_effects=True, vmem_limit_bytes=56 * 1024 * 1024
        ),
    )(
        listed_blocks[0, 0],
        valid_count[0, 0],
        level_kernel[0],
        shaped,
        position[0, 0],
        observations[0, 0],
        precision[0, 0],
    )
    return result.transpose(0, 2, 1, 3).reshape(ensemble.shape)


def solution(mesh):
    placed = (
        P("member", "patch", None, "level", None, None),
        P("patch", "member", None, None),
        P("patch", "member", None, None),
        P("patch", "member", None),
        P("patch", "member", None, None),
        P("level", None),
        P("patch", "member", None),
    )
    return jax.shard_map(
        body,
        mesh=mesh,
        in_specs=placed,
        out_specs=P("member", "patch", None, "level", None, None),
        check_vma=False,
    )
```

```python
import functools

import jax
import jax.numpy as jnp
from jax import lax
from jax.experimental import pallas as pl
from jax.experimental.pallas import tpu as pltpu
from jax.sharding import PartitionSpec as P

VARIABLES = 12
COLUMNS = 1024
SLOTS = 128
OWN_BLOCKS = 2
LISTED = 8
SWEEPS = 6

MESH = pl.DeviceIdType.MESH
exact_precision = lax.Precision.HIGHEST


def wait_bytes(ref, sem):
    pltpu.make_async_copy(ref, ref, sem).wait()


def kernel(
    n,
    rows,
    lead,
    listed_ref,
    valid_ref,
    level_ref,
    ensemble_ref,
    position_ref,
    observed_ref,
    precision_ref,
    out_ref,
    landed,
    loaded,
    fields_ref,
    recv,
    done,
    where_ref,
    term_ref,
    other_term,
    equiv_ref,
    near,
    pairs_ref,
    near_pairs,
    scaled_ref,
    weights_ref,
    load_sem,
    recv_sem,
    send_sem,
    back_sem,
    back_send_sem,
    where_sem,
    term_sem,
    own_sem,
    row_sem,
    core_sem,
    pair_sem,
    pair_send_sem,
):
    me = lax.axis_index("member")
    row = lax.axis_index("patch")
    level = lax.axis_index("level")
    local_members = recv.shape[2]
    members = n * local_members
    sibling = (me, row, 1 - level)

    def row_inside(step):
        return (row + step >= 0) & (row + step < rows)

    def load(v, carry):
        pltpu.make_async_copy(ensemble_ref.at[:, v], loaded.at[v], load_sem.at[v]).start()
        return carry

    lax.fori_loop(0, VARIABLES, load, 0)

    barrier = pltpu.get_barrier_semaphore()
    for step in (-1, 0, 1):

        @pl.when(row_inside(step))
        def _():
            def greet(other, carry):
                @pl.when((other != me) if step == 0 else (other >= 0))
                def _():
                    pl.semaphore_signal(
                        barrier, inc=1, device_id=(other, row + step, level), device_id_type=MESH
                    )

                return carry

            lax.fori_loop(0, n, greet, 0)

    pl.semaphore_signal(barrier, inc=1, device_id=sibling, device_id_type=MESH)

    def arrange(v, carry):
        wait_bytes(loaded.at[v], load_sem.at[v])
        turned = jnp.transpose(loaded[v].astype(jnp.float32), (1, 0, 2))
        fields_ref[v] = turned.astype(jnp.bfloat16)
        return carry

    arrange(0, 0)
    row_count = 1 + jnp.where(row > 0, 1, 0) + jnp.where(row < rows - 1, 1, 0)
    pl.semaphore_wait(barrier, row_count * n)

    where_ref[me] = jnp.zeros(where_ref.shape[1:], where_ref.dtype)
    where_ref[me, 0:OWN_BLOCKS] = position_ref[...]

    def send_where(shift, carry):
        pltpu.make_async_remote_copy(
            src_ref=where_ref.at[me],
            dst_ref=where_ref.at[me],
            send_sem=where_sem.at[0],
            recv_sem=where_sem.at[1],
            device_id=(lax.rem(me + shift, n), row, level),
            device_id_type=MESH,
        ).start()
        return carry

    lax.fori_loop(1, n, send_where, 0)

    def send_fields(v, carry):
        def send(shift, inner):
            other = lax.rem(me + shift, n)
            pltpu.make_async_remote_copy(
                src_ref=fields_ref.at[v, other],
                dst_ref=recv.at[v, me],
                send_sem=send_sem.at[v],
                recv_sem=recv_sem.at[v],
                device_id=(other, row, level),
                device_id_type=MESH,
            ).start()
            return inner

        lax.fori_loop(1, n, send, 0)
        pltpu.make_async_copy(fields_ref.at[v, me], recv.at[v, me], recv_sem.at[v]).start()
        return carry

    send_fields(0, 0)

    slot_index = lax.broadcasted_iota(jnp.int32, (1, SLOTS), 1)
    pairs_ref[...] = jnp.zeros(pairs_ref.shape, pairs_ref.dtype)
    for block in range(OWN_BLOCKS):
        pairs_ref[block] = observed_ref[block]
        kept = jnp.where(slot_index < valid_ref[block], precision_ref[block : block + 1], 0.0)
        pairs_ref[OWN_BLOCKS + block : OWN_BLOCKS + block + 1] = kept

    def pair_copy(step, shift):
        return pltpu.make_async_remote_copy(
            src_ref=pairs_ref,
            dst_ref=near_pairs.at[1 - step, 1 - shift],
            send_sem=pair_send_sem.at[1 - step, 1 - shift],
            recv_sem=pair_sem.at[1 - step, 1 - shift],
            device_id=(me + shift, row + step, level),
            device_id_type=MESH,
        )

    def pair_inside(step, shift):
        return row_inside(step) & (me + shift >= 0) & (me + shift < n)

    ring = [(a, b) for a in (-1, 0, 1) for b in (-1, 0, 1) if (a, b) != (0, 0)]
    for step, shift in ring:

        @pl.when(pair_inside(step, shift))
        def _():
            pair_copy(step, shift).start()

        @pl.when(jnp.logical_not(pair_inside(step, shift)))
        def _():
            near_pairs[1 + step, 1 + shift] = jnp.zeros(near_pairs.shape[2:], near_pairs.dtype)

    near_pairs[1, 1] = pairs_ref[...]

    def arrange_and_send(v, carry):
        return send_fields(v, arrange(v, carry))

    lax.fori_loop(1, lead, arrange_and_send, 0)
    lax.fori_loop(lead, VARIABLES, arrange, 0)

    wait_bytes(where_ref.at[pl.ds(0, n - 1)], where_sem.at[1])
    column_iota = lax.broadcasted_iota(jnp.int32, (COLUMNS, OWN_BLOCKS * SLOTS), 0)

    def observe(p, carry):
        where = where_ref[p]
        where = jnp.concatenate([where[b : b + 1] for b in range(OWN_BLOCKS)], axis=1)
        variable_of = where // COLUMNS
        hot = jnp.where(where - variable_of * COLUMNS == column_iota, 1.0, 0.0)
        fields = fields_ref[:, p]
        if local_members % 16:
            fields = fields.astype(jnp.float32)
        fields = fields.reshape(VARIABLES * local_members, COLUMNS).astype(jnp.bfloat16)
        spread = jnp.dot(fields, hot.astype(jnp.bfloat16), preferred_element_type=jnp.float32)
        total = jnp.zeros((local_members, OWN_BLOCKS * SLOTS), jnp.float32)
        for v in range(VARIABLES):
            factor = jnp.where(variable_of == v, level_ref[v], 0.0)
            total = total + spread[v * local_members : (v + 1) * local_members] * factor
        for b in range(OWN_BLOCKS):
            term_ref[b, p] = total[:, b * SLOTS : (b + 1) * SLOTS]
        return carry

    lax.fori_loop(0, n, observe, 0)
    term_copy = pltpu.make_async_remote_copy(
        src_ref=term_ref.at[1 - level],
        dst_ref=other_term,
        send_sem=term_sem.at[0],
        recv_sem=term_sem.at[1],
        device_id=sibling,
        device_id_type=MESH,
    )
    term_copy.start()
    lax.fori_loop(lead, lead + 1, send_fields, 0)
    term_copy.wait_recv()
    equiv_ref[0] = jnp.zeros(equiv_ref.shape[1:], equiv_ref.dtype)
    equiv_ref[n + 1] = jnp.zeros(equiv_ref.shape[1:], equiv_ref.dtype)

    def add_levels(p, carry):
        equiv_ref[p + 1] = (term_ref[level, p] + other_term[p]).astype(jnp.bfloat16)
        return carry

    lax.fori_loop(0, n, add_levels, 0)

    def send_own(shift, carry):
        other = lax.rem(me + shift, n)
        pltpu.make_async_remote_copy(
            src_ref=equiv_ref.at[pl.ds(other, 3)],
            dst_ref=near.at[level, 1, me],
            send_sem=own_sem.at[0],
            recv_sem=own_sem.at[1],
            device_id=(other, row, level),
            device_id_type=MESH,
        ).start()
        return carry

    lax.fori_loop(1, n, send_own, 0)
    pltpu.make_async_copy(
        equiv_ref.at[pl.ds(me, 3)], near.at[level, 1, me], own_sem.at[1]
    ).start()
    lax.fori_loop(lead + 1, lead + 2, send_fields, 0)
    wait_bytes(near.at[level, 1], own_sem.at[1])

    def row_copy(step):
        return pltpu.make_async_remote_copy(
            src_ref=near.at[level, 1],
            dst_ref=near.at[level, 1 - step],
            send_sem=row_sem.at[0, 1 - step],
            recv_sem=row_sem.at[1, 1 - step],
            device_id=(me, row + step, level),
            device_id_type=MESH,
        )

    for step in (-1, 1):

        @pl.when(row_inside(step))
        def _():
            row_copy(step).start()

        @pl.when(jnp.logical_not(row_inside(step)))
        def _():
            near[level, 1 + step] = jnp.zeros(near.shape[2:], near.dtype)

    lax.fori_loop(lead + 2, lead + 3, send_fields, 0)
    for step in (-1, 1):

        @pl.when(row_inside(step))
        def _():
            wait_bytes(near.at[level, 1 + step], row_sem.at[1, 1 + step])

    core_copy = pltpu.make_async_remote_copy(
        src_ref=near.at[level],
        dst_ref=near.at[level],
        send_sem=core_sem.at[0],
        recv_sem=core_sem.at[1],
        device_id=sibling,
        device_id_type=MESH,
    )
    core_copy.start()
    lax.fori_loop(lead + 3, VARIABLES, send_fields, 0)
    wait_bytes(near.at[1 - level], core_sem.at[1])

    for step, shift in ring:

        @pl.when(pair_inside(step, shift))
        def _():
            wait_bytes(near_pairs.at[1 + step, 1 + shift], pair_sem.at[1 + step, 1 + shift])

    def gather(entry, forcing):
        candidate = listed_ref[entry]
        place = candidate // OWN_BLOCKS
        block = candidate % OWN_BLOCKS
        down = place // 3
        across = place % 3
        moved = jnp.abs(down - 1) + jnp.abs(across - 1)
        taper = jnp.where(moved == 0, 1.0, jnp.where(moved == 1, 0.6, 0.35)).astype(jnp.float32)
        chosen = near[block, down, :, across].astype(jnp.float32).reshape(members, SLOTS)
        pairs = near_pairs[down, across]
        seen = jnp.where(block == 0, pairs[0:1], pairs[1:2])
        weight = jnp.where(block == 0, pairs[2:3], pairs[3:4]) * taper
        centre = jnp.sum(chosen, axis=0, keepdims=True) * (1.0 / members)
        pert = (chosen - centre).astype(jnp.bfloat16).astype(jnp.float32)
        scaled_ref[entry] = (pert * jnp.sqrt(weight)).astype(jnp.bfloat16)
        return forcing + jnp.sum(pert * (weight * (seen - centre)), axis=1, keepdims=True)

    forcing = lax.fori_loop(0, LISTED, gather, jnp.zeros((members, 1), jnp.float32))
    same = lax.broadcasted_iota(jnp.int32, (members, members), 0) == lax.broadcasted_iota(
        jnp.int32, (members, members), 1
    )
    identity = jnp.where(same, 1.0, 0.0).astype(jnp.float32)

    def outer(entry, system):
        part = scaled_ref[entry]
        return system + lax.dot_general(
            part, part, (((1,), (1,)), ((), ())), preferred_element_type=jnp.float32
        )

    system = lax.fori_loop(0, LISTED, outer, (members - 1) / 1.1 * identity)
    square = jnp.sum(jnp.sum(system * system, axis=1, keepdims=True), axis=0, keepdims=True)
    scaling = jnp.sqrt(square)

    def exact(a, b):
        return jnp.dot(a, b, precision=exact_precision, preferred_element_type=jnp.float32)

    def halves(a):
        high = a.astype(jnp.bfloat16)
        return high, (a - high.astype(jnp.float32)).astype(jnp.bfloat16)

    def product(a, b):
        (a_high, a_low), (b_high, b_low) = a, b
        return jnp.dot(
            jnp.concatenate([a_low, a_high, a_high], axis=1),
            jnp.concatenate([b_high, b_low, b_high], axis=0),
            preferred_element_type=jnp.float32,
        )

    def sweep(_, carry):
        iterate, inverse_root = carry
        iterate_parts, root_parts = halves(iterate), halves(inverse_root)
        middle = halves(1.5 * identity - 0.5 * product(root_parts, iterate_parts))
        return product(iterate_parts, middle), product(middle, root_parts)

    iterate = system / scaling
    inverse_root = 1.5 * identity - 0.5 * iterate
    iterate = product(halves(iterate), halves(inverse_root))
    iterate, inverse_root = lax.fori_loop(1, SWEEPS - 1, sweep, (iterate, inverse_root))
    root_parts = halves(inverse_root)
    middle = 1.5 * identity - 0.5 * product(root_parts, halves(iterate))
    inverse_root = product(halves(middle), root_parts)
    wide = jnp.broadcast_to(forcing, (members, SLOTS))
    mean_weight = exact(inverse_root, exact(inverse_root, wide))[:, 0:1] / scaling
    weights = jnp.sqrt((members - 1) / scaling) * inverse_root + mean_weight
    weights_ref[...] = weights.T.astype(jnp.bfloat16)

    def apply(v, carry):
        wait_bytes(recv.at[v], recv_sem.at[v])
        fields = recv[v].astype(jnp.float32).reshape(members, COLUMNS)
        mean = jnp.sum(fields, axis=0, keepdims=True) * (1.0 / members)
        pert = (fields - mean).astype(jnp.bfloat16)
        updated = jnp.dot(weights_ref[...], pert, preferred_element_type=jnp.float32) + mean
        done[v] = updated.reshape(done.shape[1:]).astype(done.dtype)

        def send(shift, inner):
            other = lax.rem(me + shift, n)
            pltpu.make_async_remote_copy(
                src_ref=done.at[v, other],
                dst_ref=landed.at[v, me],
                send_sem=back_send_sem.at[v],
                recv_sem=back_sem.at[v],
                device_id=(other, row, level),
                device_id_type=MESH,
            ).start()
            return inner

        lax.fori_loop(1, n, send, 0)
        pltpu.make_async_copy(done.at[v, me], landed.at[v, me], back_sem.at[v]).start()
        return carry

    lax.fori_loop(0, VARIABLES, apply, 0)

    def restore(v, carry):
        wait_bytes(landed.at[v], back_sem.at[v])
        turned = jnp.transpose(landed[v].astype(jnp.float32), (1, 0, 2))
        loaded[v] = turned.astype(jnp.bfloat16)
        pltpu.make_async_copy(loaded.at[v], out_ref.at[:, v], load_sem.at[v]).start()
        return carry


    lax.fori_loop(0, VARIABLES, restore, 0)
    wait_bytes(where_ref.at[pl.ds(0, n - 1)], where_sem.at[0])
    term_copy.wait_send()
    wait_bytes(near.at[0, 1, pl.ds(0, n - 1)], own_sem.at[0])
    for step in (-1, 1):

        @pl.when(row_inside(step))
        def _():
            row_copy(step).wait_send()

    core_copy.wait_send()
    for step, shift in ring:

        @pl.when(pair_inside(step, shift))
        def _():
            pair_copy(step, shift).wait_send()

    def finish(v, carry):
        wait_bytes(recv.at[v, pl.ds(0, n - 1)], send_sem.at[v])
        wait_bytes(done.at[v, pl.ds(0, n - 1)], back_send_sem.at[v])
        wait_bytes(loaded.at[v], load_sem.at[v])
        return carry

    lax.fori_loop(0, VARIABLES, finish, 0)


def hand_over(result_ref, out_ref, sem):
    def piece(v):
        return pltpu.make_async_copy(result_ref.at[:, v], out_ref.at[:, v], sem.at[v])

    for v in range(VARIABLES):
        piece(v).start()
    for v in range(VARIABLES):
        piece(v).wait()


def body(ensemble, observations, precision, valid_count, position, level_kernel, listed_blocks):
    n = lax.axis_size("member")
    rows = lax.axis_size("patch")
    local_members = ensemble.shape[0]
    members = local_members * n
    lead = 4
    shaped = ensemble.reshape(local_members, n, VARIABLES, COLUMNS).transpose(0, 2, 1, 3)
    parts = (VARIABLES, n, local_members, COLUMNS)
    sem = pltpu.SemaphoreType.DMA
    smem = pl.BlockSpec(memory_space=pltpu.SMEM)
    vmem = pl.BlockSpec(memory_space=pltpu.VMEM)
    whole = pl.BlockSpec(memory_space=pl.ANY)
    result = pl.pallas_call(
        functools.partial(kernel, n, rows, lead),
        out_shape=jax.ShapeDtypeStruct(shaped.shape, jnp.bfloat16),
        in_specs=[smem, smem, smem, whole, vmem, vmem, vmem],
        out_specs=whole,
        scratch_shapes=[
            pltpu.VMEM(parts, jnp.bfloat16),
            pltpu.VMEM((VARIABLES, local_members, n, COLUMNS), jnp.bfloat16),
            pltpu.VMEM(parts, jnp.bfloat16),
            pltpu.VMEM(parts, jnp.bfloat16),
            pltpu.VMEM(parts, jnp.bfloat16),
            pltpu.VMEM((n, 8, SLOTS), jnp.int32),
            pltpu.VMEM((OWN_BLOCKS, n, local_members, SLOTS), jnp.float32),
            pltpu.VMEM((n, local_members, SLOTS), jnp.float32),
            pltpu.VMEM((n + 2, local_members, SLOTS), jnp.bfloat16),
            pltpu.VMEM((OWN_BLOCKS, 3, n, 3, local_members, SLOTS), jnp.bfloat16),
            pltpu.VMEM((8, SLOTS), jnp.float32),
            pltpu.VMEM((3, 3, 8, SLOTS), jnp.float32),
            pltpu.VMEM((LISTED, members, SLOTS), jnp.bfloat16),
            pltpu.VMEM((members, members), jnp.bfloat16),
            sem((VARIABLES,)),
            sem((VARIABLES,)),
            sem((VARIABLES,)),
            sem((VARIABLES,)),
            sem((VARIABLES,)),
            sem((2,)),
            sem((2,)),
            sem((2,)),
            sem((2, 3)),
            sem((2,)),
            sem((3, 3)),
            sem((3, 3)),
        ],
        compiler_params=pltpu.CompilerParams(
            collective_id=0, has_side_effects=True, vmem_limit_bytes=56 * 1024 * 1024
        ),
    )(
        listed_blocks[0, 0],
        valid_count[0, 0],
        level_kernel[0],
        shaped,
        position[0, 0],
        observations[0, 0],
        precision[0, 0],
    )
    result = pl.pallas_call(
        hand_over,
        out_shape=jax.ShapeDtypeStruct(shaped.shape, jnp.bfloat16),
        in_specs=[whole],
        out_specs=whole,
        scratch_shapes=[sem((VARIABLES,))],
        compiler_params=pltpu.CompilerParams(vmem_limit_bytes=56 * 1024 * 1024),
    )(result)
    return result.transpose(0, 2, 1, 3).reshape(ensemble.shape)


def solution(mesh):
    placed = (
        P("member", "patch", None, "level", None, None),
        P("patch", "member", None, None),
        P("patch", "member", None, None),
        P("patch", "member", None),
        P("patch", "member", None, None),
        P("level", None),
        P("patch", "member", None),
    )
    return jax.shard_map(
        body,
        mesh=mesh,
        in_specs=placed,
        out_specs=P("member", "patch", None, "level", None, None),
        check_vma=False,
    )
```

```python
import functools

import jax
import jax.numpy as jnp
from jax import lax
from jax.experimental import pallas as pl
from jax.experimental.pallas import tpu as pltpu
from jax.sharding import PartitionSpec as P

VARIABLES = 12
COLUMNS = 1024
SLOTS = 128
OWN_BLOCKS = 2
LISTED = 8
SWEEPS = 6

MESH = pl.DeviceIdType.MESH
exact_precision = lax.Precision.HIGHEST


def wait_bytes(ref, sem):
    pltpu.make_async_copy(ref, ref, sem).wait()


def kernel(
    n,
    rows,
    lead,
    listed_ref,
    valid_ref,
    level_ref,
    ensemble_ref,
    position_ref,
    observed_ref,
    precision_ref,
    out_ref,
    landed,
    loaded,
    fields_ref,
    recv,
    done,
    where_ref,
    term_ref,
    other_term,
    equiv_ref,
    near,
    pairs_ref,
    near_pairs,
    scaled_ref,
    weights_ref,
    load_sem,
    recv_sem,
    send_sem,
    back_sem,
    back_send_sem,
    where_sem,
    term_sem,
    own_sem,
    row_sem,
    core_sem,
    pair_sem,
    pair_send_sem,
):
    me = lax.axis_index("member")
    row = lax.axis_index("patch")
    level = lax.axis_index("level")
    local_members = recv.shape[2]
    members = n * local_members
    sibling = (me, row, 1 - level)

    def row_inside(step):
        return (row + step >= 0) & (row + step < rows)

    def load(v, carry):
        pltpu.make_async_copy(ensemble_ref.at[:, v], loaded.at[v], load_sem.at[v]).start()
        return carry

    lax.fori_loop(0, VARIABLES, load, 0)

    barrier = pltpu.get_barrier_semaphore()
    for step in (-1, 0, 1):

        @pl.when(row_inside(step))
        def _():
            def greet(other, carry):
                @pl.when((other != me) if step == 0 else (other >= 0))
                def _():
                    pl.semaphore_signal(
                        barrier, inc=1, device_id=(other, row + step, level), device_id_type=MESH
                    )

                return carry

            lax.fori_loop(0, n, greet, 0)

    pl.semaphore_signal(barrier, inc=1, device_id=sibling, device_id_type=MESH)

    def arrange(v, carry):
        wait_bytes(loaded.at[v], load_sem.at[v])
        turned = jnp.transpose(loaded[v].astype(jnp.float32), (1, 0, 2))
        fields_ref[v] = turned.astype(jnp.bfloat16)
        return carry

    arrange(0, 0)
    row_count = 1 + jnp.where(row > 0, 1, 0) + jnp.where(row < rows - 1, 1, 0)
    pl.semaphore_wait(barrier, row_count * n)

    where_ref[me] = jnp.zeros(where_ref.shape[1:], where_ref.dtype)
    where_ref[me, 0:OWN_BLOCKS] = position_ref[...]

    def send_where(shift, carry):
        pltpu.make_async_remote_copy(
            src_ref=where_ref.at[me],
            dst_ref=where_ref.at[me],
            send_sem=where_sem.at[0],
            recv_sem=where_sem.at[1],
            device_id=(lax.rem(me + shift, n), row, level),
            device_id_type=MESH,
        ).start()
        return carry

    lax.fori_loop(1, n, send_where, 0)

    def send_fields(v, carry):
        def send(shift, inner):
            other = lax.rem(me + shift, n)
            pltpu.make_async_remote_copy(
                src_ref=fields_ref.at[v, other],
                dst_ref=recv.at[v, me],
                send_sem=send_sem.at[v],
                recv_sem=recv_sem.at[v],
                device_id=(other, row, level),
                device_id_type=MESH,
            ).start()
            return inner

        lax.fori_loop(1, n, send, 0)
        pltpu.make_async_copy(fields_ref.at[v, me], recv.at[v, me], recv_sem.at[v]).start()
        return carry

    send_fields(0, 0)

    slot_index = lax.broadcasted_iota(jnp.int32, (1, SLOTS), 1)
    pairs_ref[...] = jnp.zeros(pairs_ref.shape, pairs_ref.dtype)
    for block in range(OWN_BLOCKS):
        pairs_ref[block] = observed_ref[block]
        kept = jnp.where(slot_index < valid_ref[block], precision_ref[block : block + 1], 0.0)
        pairs_ref[OWN_BLOCKS + block : OWN_BLOCKS + block + 1] = kept

    def pair_copy(step, shift):
        return pltpu.make_async_remote_copy(
            src_ref=pairs_ref,
            dst_ref=near_pairs.at[1 - step, 1 - shift],
            send_sem=pair_send_sem.at[1 - step, 1 - shift],
            recv_sem=pair_sem.at[1 - step, 1 - shift],
            device_id=(me + shift, row + step, level),
            device_id_type=MESH,
        )

    def pair_inside(step, shift):
        return row_inside(step) & (me + shift >= 0) & (me + shift < n)

    ring = [(a, b) for a in (-1, 0, 1) for b in (-1, 0, 1) if (a, b) != (0, 0)]
    for step, shift in ring:

        @pl.when(pair_inside(step, shift))
        def _():
            pair_copy(step, shift).start()

        @pl.when(jnp.logical_not(pair_inside(step, shift)))
        def _():
            near_pairs[1 + step, 1 + shift] = jnp.zeros(near_pairs.shape[2:], near_pairs.dtype)

    near_pairs[1, 1] = pairs_ref[...]

    def arrange_and_send(v, carry):
        return send_fields(v, arrange(v, carry))

    lax.fori_loop(1, lead, arrange_and_send, 0)
    lax.fori_loop(lead, VARIABLES, arrange, 0)

    wait_bytes(where_ref.at[pl.ds(0, n - 1)], where_sem.at[1])
    column_iota = lax.broadcasted_iota(jnp.int32, (COLUMNS, OWN_BLOCKS * SLOTS), 0)

    def observe(p, carry):
        where = where_ref[p]
        where = jnp.concatenate([where[b : b + 1] for b in range(OWN_BLOCKS)], axis=1)
        variable_of = where // COLUMNS
        hot = jnp.where(where - variable_of * COLUMNS == column_iota, 1.0, 0.0)
        fields = fields_ref[:, p]
        if local_members % 16:
            fields = fields.astype(jnp.float32)
        fields = fields.reshape(VARIABLES * local_members, COLUMNS).astype(jnp.bfloat16)
        spread = jnp.dot(fields, hot.astype(jnp.bfloat16), preferred_element_type=jnp.float32)
        total = jnp.zeros((local_members, OWN_BLOCKS * SLOTS), jnp.float32)
        for v in range(VARIABLES):
            factor = jnp.where(variable_of == v, level_ref[v], 0.0)
            total = total + spread[v * local_members : (v + 1) * local_members] * factor
        for b in range(OWN_BLOCKS):
            term_ref[b, p] = total[:, b * SLOTS : (b + 1) * SLOTS]
        return carry

    lax.fori_loop(0, n, observe, 0)
    term_copy = pltpu.make_async_remote_copy(
        src_ref=term_ref.at[1 - level],
        dst_ref=other_term,
        send_sem=term_sem.at[0],
        recv_sem=term_sem.at[1],
        device_id=sibling,
        device_id_type=MESH,
    )
    term_copy.start()
    lax.fori_loop(lead, lead + 1, send_fields, 0)
    term_copy.wait_recv()
    equiv_ref[0] = jnp.zeros(equiv_ref.shape[1:], equiv_ref.dtype)
    equiv_ref[n + 1] = jnp.zeros(equiv_ref.shape[1:], equiv_ref.dtype)

    def add_levels(p, carry):
        equiv_ref[p + 1] = (term_ref[level, p] + other_term[p]).astype(jnp.bfloat16)
        return carry

    lax.fori_loop(0, n, add_levels, 0)

    def send_own(shift, carry):
        other = lax.rem(me + shift, n)
        pltpu.make_async_remote_copy(
            src_ref=equiv_ref.at[pl.ds(other, 3)],
            dst_ref=near.at[level, 1, me],
            send_sem=own_sem.at[0],
            recv_sem=own_sem.at[1],
            device_id=(other, row, level),
            device_id_type=MESH,
        ).start()
        return carry

    lax.fori_loop(1, n, send_own, 0)
    pltpu.make_async_copy(
        equiv_ref.at[pl.ds(me, 3)], near.at[level, 1, me], own_sem.at[1]
    ).start()
    lax.fori_loop(lead + 1, lead + 2, send_fields, 0)
    wait_bytes(near.at[level, 1], own_sem.at[1])

    def row_copy(step):
        return pltpu.make_async_remote_copy(
            src_ref=near.at[level, 1],
            dst_ref=near.at[level, 1 - step],
            send_sem=row_sem.at[0, 1 - step],
            recv_sem=row_sem.at[1, 1 - step],
            device_id=(me, row + step, level),
            device_id_type=MESH,
        )

    for step in (-1, 1):

        @pl.when(row_inside(step))
        def _():
            row_copy(step).start()

        @pl.when(jnp.logical_not(row_inside(step)))
        def _():
            near[level, 1 + step] = jnp.zeros(near.shape[2:], near.dtype)

    lax.fori_loop(lead + 2, lead + 3, send_fields, 0)
    for step in (-1, 1):

        @pl.when(row_inside(step))
        def _():
            wait_bytes(near.at[level, 1 + step], row_sem.at[1, 1 + step])

    core_copy = pltpu.make_async_remote_copy(
        src_ref=near.at[level],
        dst_ref=near.at[level],
        send_sem=core_sem.at[0],
        recv_sem=core_sem.at[1],
        device_id=sibling,
        device_id_type=MESH,
    )
    core_copy.start()
    lax.fori_loop(lead + 3, VARIABLES, send_fields, 0)
    wait_bytes(near.at[1 - level], core_sem.at[1])

    for step, shift in ring:

        @pl.when(pair_inside(step, shift))
        def _():
            wait_bytes(near_pairs.at[1 + step, 1 + shift], pair_sem.at[1 + step, 1 + shift])

    def gather(entry, forcing):
        candidate = listed_ref[entry]
        place = candidate // OWN_BLOCKS
        block = candidate % OWN_BLOCKS
        down = place // 3
        across = place % 3
        moved = jnp.abs(down - 1) + jnp.abs(across - 1)
        taper = jnp.where(moved == 0, 1.0, jnp.where(moved == 1, 0.6, 0.35)).astype(jnp.float32)
        chosen = near[block, down, :, across].astype(jnp.float32).reshape(members, SLOTS)
        pairs = near_pairs[down, across]
        seen = jnp.where(block == 0, pairs[0:1], pairs[1:2])
        weight = jnp.where(block == 0, pairs[2:3], pairs[3:4]) * taper
        centre = jnp.sum(chosen, axis=0, keepdims=True) * (1.0 / members)
        pert = (chosen - centre).astype(jnp.bfloat16).astype(jnp.float32)
        scaled_ref[entry] = (pert * jnp.sqrt(weight)).astype(jnp.bfloat16)
        return forcing + jnp.sum(pert * (weight * (seen - centre)), axis=1, keepdims=True)

    forcing = lax.fori_loop(0, LISTED, gather, jnp.zeros((members, 1), jnp.float32))
    same = lax.broadcasted_iota(jnp.int32, (members, members), 0) == lax.broadcasted_iota(
        jnp.int32, (members, members), 1
    )
    identity = jnp.where(same, 1.0, 0.0).astype(jnp.float32)

    def outer(entry, system):
        part = scaled_ref[entry]
        return system + lax.dot_general(
            part, part, (((1,), (1,)), ((), ())), preferred_element_type=jnp.float32
        )

    system = lax.fori_loop(0, LISTED, outer, (members - 1) / 1.1 * identity)
    square = jnp.sum(jnp.sum(system * system, axis=1, keepdims=True), axis=0, keepdims=True)
    scaling = jnp.sqrt(square)

    def exact(a, b):
        return jnp.dot(a, b, precision=exact_precision, preferred_element_type=jnp.float32)

    def halves(a):
        high = a.astype(jnp.bfloat16)
        return high, (a - high.astype(jnp.float32)).astype(jnp.bfloat16)

    def product(a, b):
        (a_high, a_low), (b_high, b_low) = a, b
        return jnp.dot(
            jnp.concatenate([a_low, a_high, a_high], axis=1),
            jnp.concatenate([b_high, b_low, b_high], axis=0),
            preferred_element_type=jnp.float32,
        )

    def sweep(_, carry):
        iterate, inverse_root = carry
        iterate_parts, root_parts = halves(iterate), halves(inverse_root)
        middle = halves(1.5 * identity - 0.5 * product(root_parts, iterate_parts))
        return product(iterate_parts, middle), product(middle, root_parts)

    iterate = system / scaling
    inverse_root = 1.5 * identity - 0.5 * iterate
    iterate = product(halves(iterate), halves(inverse_root))
    iterate, inverse_root = lax.fori_loop(1, SWEEPS - 1, sweep, (iterate, inverse_root))
    root_parts = halves(inverse_root)
    middle = 1.5 * identity - 0.5 * product(root_parts, halves(iterate))
    inverse_root = product(halves(middle), root_parts)
    wide = jnp.broadcast_to(forcing, (members, SLOTS))
    mean_weight = exact(inverse_root, exact(inverse_root, wide))[:, 0:1] / scaling
    weights = jnp.sqrt((members - 1) / scaling) * inverse_root + mean_weight
    weights_ref[...] = weights.T.astype(jnp.bfloat16)

    def apply(v, carry):
        wait_bytes(recv.at[v], recv_sem.at[v])
        fields = recv[v].astype(jnp.float32).reshape(members, COLUMNS)
        mean = jnp.sum(fields, axis=0, keepdims=True) * (1.0 / members)
        pert = (fields - mean).astype(jnp.bfloat16)
        updated = jnp.dot(weights_ref[...], pert, preferred_element_type=jnp.float32) + mean
        done[v] = updated.reshape(done.shape[1:]).astype(done.dtype)

        def send(shift, inner):
            other = lax.rem(me + shift, n)
            pltpu.make_async_remote_copy(
                src_ref=done.at[v, other],
                dst_ref=landed.at[v, me],
                send_sem=back_send_sem.at[v],
                recv_sem=back_sem.at[v],
                device_id=(other, row, level),
                device_id_type=MESH,
            ).start()
            return inner

        lax.fori_loop(1, n, send, 0)
        pltpu.make_async_copy(done.at[v, me], landed.at[v, me], back_sem.at[v]).start()
        return carry

    lax.fori_loop(0, VARIABLES, apply, 0)

    def restore(v, carry):
        wait_bytes(landed.at[v], back_sem.at[v])
        turned = jnp.transpose(landed[v].astype(jnp.float32), (1, 0, 2))
        out_ref[:, v] = turned.astype(jnp.bfloat16)
        return carry


    lax.fori_loop(0, VARIABLES, restore, 0)
    wait_bytes(where_ref.at[pl.ds(0, n - 1)], where_sem.at[0])
    term_copy.wait_send()
    wait_bytes(near.at[0, 1, pl.ds(0, n - 1)], own_sem.at[0])
    for step in (-1, 1):

        @pl.when(row_inside(step))
        def _():
            row_copy(step).wait_send()

    core_copy.wait_send()
    for step, shift in ring:

        @pl.when(pair_inside(step, shift))
        def _():
            pair_copy(step, shift).wait_send()

    def finish(v, carry):
        wait_bytes(recv.at[v, pl.ds(0, n - 1)], send_sem.at[v])
        wait_bytes(done.at[v, pl.ds(0, n - 1)], back_send_sem.at[v])
        return carry

    lax.fori_loop(0, VARIABLES, finish, 0)


def hand_over(result_ref, out_ref, sem):
    pieces = sem.shape[0]
    held = result_ref.shape[0] // pieces

    def piece(place):
        part = pl.ds(place * held, held)
        return pltpu.make_async_copy(result_ref.at[part], out_ref.at[part], sem.at[place])

    for place in range(pieces):
        piece(place).start()
    for place in range(pieces):
        piece(place).wait()


def body(ensemble, observations, precision, valid_count, position, level_kernel, listed_blocks):
    n = lax.axis_size("member")
    rows = lax.axis_size("patch")
    local_members = ensemble.shape[0]
    members = local_members * n
    lead = 4
    shaped = ensemble.reshape(local_members, n, VARIABLES, COLUMNS).transpose(0, 2, 1, 3)
    parts = (VARIABLES, n, local_members, COLUMNS)
    sem = pltpu.SemaphoreType.DMA
    smem = pl.BlockSpec(memory_space=pltpu.SMEM)
    vmem = pl.BlockSpec(memory_space=pltpu.VMEM)
    whole = pl.BlockSpec(memory_space=pl.ANY)
    result = pl.pallas_call(
        functools.partial(kernel, n, rows, lead),
        out_shape=jax.ShapeDtypeStruct(shaped.shape, jnp.bfloat16),
        in_specs=[smem, smem, smem, whole, vmem, vmem, vmem],
        out_specs=vmem,
        scratch_shapes=[
            pltpu.VMEM(parts, jnp.bfloat16),
            pltpu.VMEM((VARIABLES, local_members, n, COLUMNS), jnp.bfloat16),
            pltpu.VMEM(parts, jnp.bfloat16),
            pltpu.VMEM(parts, jnp.bfloat16),
            pltpu.VMEM(parts, jnp.bfloat16),
            pltpu.VMEM((n, 8, SLOTS), jnp.int32),
            pltpu.VMEM((OWN_BLOCKS, n, local_members, SLOTS), jnp.float32),
            pltpu.VMEM((n, local_members, SLOTS), jnp.float32),
            pltpu.VMEM((n + 2, local_members, SLOTS), jnp.bfloat16),
            pltpu.VMEM((OWN_BLOCKS, 3, n, 3, local_members, SLOTS), jnp.bfloat16),
            pltpu.VMEM((8, SLOTS), jnp.float32),
            pltpu.VMEM((3, 3, 8, SLOTS), jnp.float32),
            pltpu.VMEM((LISTED, members, SLOTS), jnp.bfloat16),
            pltpu.VMEM((members, members), jnp.bfloat16),
            sem((VARIABLES,)),
            sem((VARIABLES,)),
            sem((VARIABLES,)),
            sem((VARIABLES,)),
            sem((VARIABLES,)),
            sem((2,)),
            sem((2,)),
            sem((2,)),
            sem((2, 3)),
            sem((2,)),
            sem((3, 3)),
            sem((3, 3)),
        ],
        compiler_params=pltpu.CompilerParams(
            collective_id=0, has_side_effects=True, vmem_limit_bytes=42 * 1024 * 1024
        ),
    )(
        listed_blocks[0, 0],
        valid_count[0, 0],
        level_kernel[0],
        shaped,
        position[0, 0],
        observations[0, 0],
        precision[0, 0],
    )
    result = pl.pallas_call(
        hand_over,
        out_shape=jax.ShapeDtypeStruct(shaped.shape, jnp.bfloat16),
        in_specs=[whole],
        out_specs=whole,
        scratch_shapes=[sem((4,))],
    )(result)
    return result.transpose(0, 2, 1, 3).reshape(ensemble.shape)


def solution(mesh):
    placed = (
        P("member", "patch", None, "level", None, None),
        P("patch", "member", None, None),
        P("patch", "member", None, None),
        P("patch", "member", None),
        P("patch", "member", None, None),
        P("level", None),
        P("patch", "member", None),
    )
    return jax.shard_map(
        body,
        mesh=mesh,
        in_specs=placed,
        out_specs=P("member", "patch", None, "level", None, None),
        check_vma=False,
    )
```

```python
import functools

import jax
import jax.numpy as jnp
from jax import lax
from jax.experimental import pallas as pl
from jax.experimental.pallas import tpu as pltpu
from jax.sharding import PartitionSpec as P

VARIABLES = 12
COLUMNS = 1024
SLOTS = 128
OWN_BLOCKS = 2
LISTED = 8
SWEEPS = 6

MESH = pl.DeviceIdType.MESH
exact_precision = lax.Precision.HIGHEST


def wait_bytes(ref, sem):
    pltpu.make_async_copy(ref, ref, sem).wait()


def kernel(
    n,
    rows,
    lead,
    listed_ref,
    valid_ref,
    level_ref,
    ensemble_ref,
    position_ref,
    observed_ref,
    precision_ref,
    out_ref,
    landed,
    loaded,
    fields_ref,
    recv,
    done,
    where_ref,
    term_ref,
    other_term,
    equiv_ref,
    near,
    pairs_ref,
    near_pairs,
    scaled_ref,
    weights_ref,
    load_sem,
    recv_sem,
    send_sem,
    back_sem,
    back_send_sem,
    where_sem,
    term_sem,
    own_sem,
    row_sem,
    core_sem,
    pair_sem,
    pair_send_sem,
):
    me = lax.axis_index("member")
    row = lax.axis_index("patch")
    level = lax.axis_index("level")
    local_members = recv.shape[2]
    members = n * local_members
    sibling = (me, row, 1 - level)

    def row_inside(step):
        return (row + step >= 0) & (row + step < rows)

    def load(v, carry):
        pltpu.make_async_copy(ensemble_ref.at[:, v], loaded.at[v], load_sem.at[v]).start()
        return carry

    lax.fori_loop(0, VARIABLES, load, 0)

    barrier = pltpu.get_barrier_semaphore()
    for step in (-1, 0, 1):

        @pl.when(row_inside(step))
        def _():
            def greet(other, carry):
                @pl.when((other != me) if step == 0 else (other >= 0))
                def _():
                    pl.semaphore_signal(
                        barrier, inc=1, device_id=(other, row + step, level), device_id_type=MESH
                    )

                return carry

            lax.fori_loop(0, n, greet, 0)

    pl.semaphore_signal(barrier, inc=1, device_id=sibling, device_id_type=MESH)

    def arrange(v, carry):
        wait_bytes(loaded.at[v], load_sem.at[v])
        turned = jnp.transpose(loaded[v].astype(jnp.float32), (1, 0, 2))
        fields_ref[v] = turned.astype(jnp.bfloat16)
        return carry

    arrange(0, 0)
    row_count = 1 + jnp.where(row > 0, 1, 0) + jnp.where(row < rows - 1, 1, 0)
    pl.semaphore_wait(barrier, row_count * n)

    where_ref[me] = jnp.zeros(where_ref.shape[1:], where_ref.dtype)
    where_ref[me, 0:OWN_BLOCKS] = position_ref[...]

    def send_where(shift, carry):
        pltpu.make_async_remote_copy(
            src_ref=where_ref.at[me],
            dst_ref=where_ref.at[me],
            send_sem=where_sem.at[0],
            recv_sem=where_sem.at[1],
            device_id=(lax.rem(me + shift, n), row, level),
            device_id_type=MESH,
        ).start()
        return carry

    lax.fori_loop(1, n, send_where, 0)

    def send_fields(v, carry):
        def send(shift, inner):
            other = lax.rem(me + shift, n)
            pltpu.make_async_remote_copy(
                src_ref=fields_ref.at[v, other],
                dst_ref=recv.at[v, me],
                send_sem=send_sem.at[v],
                recv_sem=recv_sem.at[v],
                device_id=(other, row, level),
                device_id_type=MESH,
            ).start()
            return inner

        lax.fori_loop(1, n, send, 0)
        pltpu.make_async_copy(fields_ref.at[v, me], recv.at[v, me], recv_sem.at[v]).start()
        return carry

    send_fields(0, 0)

    slot_index = lax.broadcasted_iota(jnp.int32, (1, SLOTS), 1)
    pairs_ref[...] = jnp.zeros(pairs_ref.shape, pairs_ref.dtype)
    for block in range(OWN_BLOCKS):
        pairs_ref[block] = observed_ref[block]
        kept = jnp.where(slot_index < valid_ref[block], precision_ref[block : block + 1], 0.0)
        pairs_ref[OWN_BLOCKS + block : OWN_BLOCKS + block + 1] = kept

    def pair_copy(step, shift):
        return pltpu.make_async_remote_copy(
            src_ref=pairs_ref,
            dst_ref=near_pairs.at[1 - step, 1 - shift],
            send_sem=pair_send_sem.at[1 - step, 1 - shift],
            recv_sem=pair_sem.at[1 - step, 1 - shift],
            device_id=(me + shift, row + step, level),
            device_id_type=MESH,
        )

    def pair_inside(step, shift):
        return row_inside(step) & (me + shift >= 0) & (me + shift < n)

    ring = [(a, b) for a in (-1, 0, 1) for b in (-1, 0, 1) if (a, b) != (0, 0)]
    for step, shift in ring:

        @pl.when(pair_inside(step, shift))
        def _():
            pair_copy(step, shift).start()

        @pl.when(jnp.logical_not(pair_inside(step, shift)))
        def _():
            near_pairs[1 + step, 1 + shift] = jnp.zeros(near_pairs.shape[2:], near_pairs.dtype)

    near_pairs[1, 1] = pairs_ref[...]

    def arrange_and_send(v, carry):
        return send_fields(v, arrange(v, carry))

    lax.fori_loop(1, lead, arrange_and_send, 0)
    lax.fori_loop(lead, VARIABLES, arrange, 0)

    wait_bytes(where_ref.at[pl.ds(0, n - 1)], where_sem.at[1])
    column_iota = lax.broadcasted_iota(jnp.int32, (COLUMNS, OWN_BLOCKS * SLOTS), 0)

    def observe(p, carry):
        where = where_ref[p]
        where = jnp.concatenate([where[b : b + 1] for b in range(OWN_BLOCKS)], axis=1)
        variable_of = where // COLUMNS
        hot = jnp.where(where - variable_of * COLUMNS == column_iota, 1.0, 0.0)
        fields = fields_ref[:, p]
        if local_members % 16:
            fields = fields.astype(jnp.float32)
        fields = fields.reshape(VARIABLES * local_members, COLUMNS).astype(jnp.bfloat16)
        spread = jnp.dot(fields, hot.astype(jnp.bfloat16), preferred_element_type=jnp.float32)
        total = jnp.zeros((local_members, OWN_BLOCKS * SLOTS), jnp.float32)
        for v in range(VARIABLES):
            factor = jnp.where(variable_of == v, level_ref[v], 0.0)
            total = total + spread[v * local_members : (v + 1) * local_members] * factor
        for b in range(OWN_BLOCKS):
            term_ref[b, p] = total[:, b * SLOTS : (b + 1) * SLOTS]
        return carry

    lax.fori_loop(0, n, observe, 0)
    term_copy = pltpu.make_async_remote_copy(
        src_ref=term_ref.at[1 - level],
        dst_ref=other_term,
        send_sem=term_sem.at[0],
        recv_sem=term_sem.at[1],
        device_id=sibling,
        device_id_type=MESH,
    )
    term_copy.start()
    lax.fori_loop(lead, lead + 1, send_fields, 0)
    term_copy.wait_recv()
    equiv_ref[0] = jnp.zeros(equiv_ref.shape[1:], equiv_ref.dtype)
    equiv_ref[n + 1] = jnp.zeros(equiv_ref.shape[1:], equiv_ref.dtype)

    def add_levels(p, carry):
        equiv_ref[p + 1] = (term_ref[level, p] + other_term[p]).astype(jnp.bfloat16)
        return carry

    lax.fori_loop(0, n, add_levels, 0)

    def send_own(shift, carry):
        other = lax.rem(me + shift, n)
        pltpu.make_async_remote_copy(
            src_ref=equiv_ref.at[pl.ds(other, 3)],
            dst_ref=near.at[level, 1, me],
            send_sem=own_sem.at[0],
            recv_sem=own_sem.at[1],
            device_id=(other, row, level),
            device_id_type=MESH,
        ).start()
        return carry

    lax.fori_loop(1, n, send_own, 0)
    pltpu.make_async_copy(
        equiv_ref.at[pl.ds(me, 3)], near.at[level, 1, me], own_sem.at[1]
    ).start()
    lax.fori_loop(lead + 1, lead + 2, send_fields, 0)
    wait_bytes(near.at[level, 1], own_sem.at[1])

    def row_copy(step):
        return pltpu.make_async_remote_copy(
            src_ref=near.at[level, 1],
            dst_ref=near.at[level, 1 - step],
            send_sem=row_sem.at[0, 1 - step],
            recv_sem=row_sem.at[1, 1 - step],
            device_id=(me, row + step, level),
            device_id_type=MESH,
        )

    for step in (-1, 1):

        @pl.when(row_inside(step))
        def _():
            row_copy(step).start()

        @pl.when(jnp.logical_not(row_inside(step)))
        def _():
            near[level, 1 + step] = jnp.zeros(near.shape[2:], near.dtype)

    lax.fori_loop(lead + 2, lead + 3, send_fields, 0)
    for step in (-1, 1):

        @pl.when(row_inside(step))
        def _():
            wait_bytes(near.at[level, 1 + step], row_sem.at[1, 1 + step])

    core_copy = pltpu.make_async_remote_copy(
        src_ref=near.at[level],
        dst_ref=near.at[level],
        send_sem=core_sem.at[0],
        recv_sem=core_sem.at[1],
        device_id=sibling,
        device_id_type=MESH,
    )
    core_copy.start()
    lax.fori_loop(lead + 3, VARIABLES, send_fields, 0)
    wait_bytes(near.at[1 - level], core_sem.at[1])

    for step, shift in ring:

        @pl.when(pair_inside(step, shift))
        def _():
            wait_bytes(near_pairs.at[1 + step, 1 + shift], pair_sem.at[1 + step, 1 + shift])

    def gather(entry, forcing):
        candidate = listed_ref[entry]
        place = candidate // OWN_BLOCKS
        block = candidate % OWN_BLOCKS
        down = place // 3
        across = place % 3
        moved = jnp.abs(down - 1) + jnp.abs(across - 1)
        taper = jnp.where(moved == 0, 1.0, jnp.where(moved == 1, 0.6, 0.35)).astype(jnp.float32)
        chosen = near[block, down, :, across].astype(jnp.float32).reshape(members, SLOTS)
        pairs = near_pairs[down, across]
        seen = jnp.where(block == 0, pairs[0:1], pairs[1:2])
        weight = jnp.where(block == 0, pairs[2:3], pairs[3:4]) * taper
        centre = jnp.sum(chosen, axis=0, keepdims=True) * (1.0 / members)
        pert = (chosen - centre).astype(jnp.bfloat16).astype(jnp.float32)
        scaled_ref[entry] = (pert * jnp.sqrt(weight)).astype(jnp.bfloat16)
        return forcing + jnp.sum(pert * (weight * (seen - centre)), axis=1, keepdims=True)

    forcing = lax.fori_loop(0, LISTED, gather, jnp.zeros((members, 1), jnp.float32))
    same = lax.broadcasted_iota(jnp.int32, (members, members), 0) == lax.broadcasted_iota(
        jnp.int32, (members, members), 1
    )
    identity = jnp.where(same, 1.0, 0.0).astype(jnp.float32)

    def outer(entry, system):
        part = scaled_ref[entry]
        return system + lax.dot_general(
            part, part, (((1,), (1,)), ((), ())), preferred_element_type=jnp.float32
        )

    system = lax.fori_loop(0, LISTED, outer, (members - 1) / 1.1 * identity)
    square = jnp.sum(jnp.sum(system * system, axis=1, keepdims=True), axis=0, keepdims=True)
    scaling = jnp.sqrt(square)

    def exact(a, b):
        return jnp.dot(a, b, precision=exact_precision, preferred_element_type=jnp.float32)

    def halves(a):
        high = a.astype(jnp.bfloat16)
        return high, (a - high.astype(jnp.float32)).astype(jnp.bfloat16)

    def product(a, b):
        (a_high, a_low), (b_high, b_low) = a, b
        return jnp.dot(
            jnp.concatenate([a_low, a_high, a_high], axis=1),
            jnp.concatenate([b_high, b_low, b_high], axis=0),
            preferred_element_type=jnp.float32,
        )

    def sweep(_, carry):
        iterate, inverse_root = carry
        iterate_parts, root_parts = halves(iterate), halves(inverse_root)
        middle = halves(1.5 * identity - 0.5 * product(root_parts, iterate_parts))
        return product(iterate_parts, middle), product(middle, root_parts)

    iterate = system / scaling
    inverse_root = 1.5 * identity - 0.5 * iterate
    iterate = product(halves(iterate), halves(inverse_root))
    iterate, inverse_root = lax.fori_loop(1, SWEEPS - 1, sweep, (iterate, inverse_root))
    root_parts = halves(inverse_root)
    middle = 1.5 * identity - 0.5 * product(root_parts, halves(iterate))
    inverse_root = product(halves(middle), root_parts)
    wide = jnp.broadcast_to(forcing, (members, SLOTS))
    mean_weight = exact(inverse_root, exact(inverse_root, wide))[:, 0:1] / scaling
    weights = jnp.sqrt((members - 1) / scaling) * inverse_root + mean_weight
    weights_ref[...] = weights.T.astype(jnp.bfloat16)

    def apply(v, carry):
        wait_bytes(recv.at[v], recv_sem.at[v])
        fields = recv[v].astype(jnp.float32).reshape(members, COLUMNS)
        mean = jnp.sum(fields, axis=0, keepdims=True) * (1.0 / members)
        pert = (fields - mean).astype(jnp.bfloat16)
        updated = jnp.dot(weights_ref[...], pert, preferred_element_type=jnp.float32) + mean
        done[v] = updated.reshape(done.shape[1:]).astype(done.dtype)

        def send(shift, inner):
            other = lax.rem(me + shift, n)
            pltpu.make_async_remote_copy(
                src_ref=done.at[v, other],
                dst_ref=landed.at[v, me],
                send_sem=back_send_sem.at[v],
                recv_sem=back_sem.at[v],
                device_id=(other, row, level),
                device_id_type=MESH,
            ).start()
            return inner

        lax.fori_loop(1, n, send, 0)
        pltpu.make_async_copy(done.at[v, me], landed.at[v, me], back_sem.at[v]).start()
        return carry

    lax.fori_loop(0, VARIABLES, apply, 0)

    def restore(v, carry):
        wait_bytes(landed.at[v], back_sem.at[v])
        turned = jnp.transpose(landed[v].astype(jnp.float32), (1, 0, 2))
        loaded[v] = turned.astype(jnp.bfloat16)
        pltpu.make_async_copy(loaded.at[v], out_ref.at[:, v], load_sem.at[v]).start()
        return carry


    lax.fori_loop(0, VARIABLES, restore, 0)
    wait_bytes(where_ref.at[pl.ds(0, n - 1)], where_sem.at[0])
    term_copy.wait_send()
    wait_bytes(near.at[0, 1, pl.ds(0, n - 1)], own_sem.at[0])
    for step in (-1, 1):

        @pl.when(row_inside(step))
        def _():
            row_copy(step).wait_send()

    core_copy.wait_send()
    for step, shift in ring:

        @pl.when(pair_inside(step, shift))
        def _():
            pair_copy(step, shift).wait_send()

    def finish(v, carry):
        wait_bytes(recv.at[v, pl.ds(0, n - 1)], send_sem.at[v])
        wait_bytes(done.at[v, pl.ds(0, n - 1)], back_send_sem.at[v])
        wait_bytes(loaded.at[v], load_sem.at[v])
        return carry

    lax.fori_loop(0, VARIABLES, finish, 0)


def hand_over(result_ref, out_ref, held_ref, load_sem, store_sem):
    pieces = load_sem.shape[0]
    length = result_ref.shape[0] // pieces

    def load(place):
        part = pl.ds(place * length, length)
        return pltpu.make_async_copy(result_ref.at[part], held_ref.at[part], load_sem.at[place])

    def store(place):
        part = pl.ds(place * length, length)
        return pltpu.make_async_copy(held_ref.at[part], out_ref.at[part], store_sem.at[place])

    for place in range(pieces):
        load(place).start()
    for place in range(pieces):
        load(place).wait()
        store(place).start()
    for place in range(pieces):
        store(place).wait()


def body(ensemble, observations, precision, valid_count, position, level_kernel, listed_blocks):
    n = lax.axis_size("member")
    rows = lax.axis_size("patch")
    local_members = ensemble.shape[0]
    members = local_members * n
    lead = 4
    shaped = ensemble.reshape(local_members, n, VARIABLES, COLUMNS).transpose(0, 2, 1, 3)
    parts = (VARIABLES, n, local_members, COLUMNS)
    sem = pltpu.SemaphoreType.DMA
    smem = pl.BlockSpec(memory_space=pltpu.SMEM)
    vmem = pl.BlockSpec(memory_space=pltpu.VMEM)
    whole = pl.BlockSpec(memory_space=pl.ANY)
    result = pl.pallas_call(
        functools.partial(kernel, n, rows, lead),
        out_shape=jax.ShapeDtypeStruct(shaped.shape, jnp.bfloat16),
        in_specs=[smem, smem, smem, whole, vmem, vmem, vmem],
        out_specs=whole,
        scratch_shapes=[
            pltpu.VMEM(parts, jnp.bfloat16),
            pltpu.VMEM((VARIABLES, local_members, n, COLUMNS), jnp.bfloat16),
            pltpu.VMEM(parts, jnp.bfloat16),
            pltpu.VMEM(parts, jnp.bfloat16),
            pltpu.VMEM(parts, jnp.bfloat16),
            pltpu.VMEM((n, 8, SLOTS), jnp.int32),
            pltpu.VMEM((OWN_BLOCKS, n, local_members, SLOTS), jnp.float32),
            pltpu.VMEM((n, local_members, SLOTS), jnp.float32),
            pltpu.VMEM((n + 2, local_members, SLOTS), jnp.bfloat16),
            pltpu.VMEM((OWN_BLOCKS, 3, n, 3, local_members, SLOTS), jnp.bfloat16),
            pltpu.VMEM((8, SLOTS), jnp.float32),
            pltpu.VMEM((3, 3, 8, SLOTS), jnp.float32),
            pltpu.VMEM((LISTED, members, SLOTS), jnp.bfloat16),
            pltpu.VMEM((members, members), jnp.bfloat16),
            sem((VARIABLES,)),
            sem((VARIABLES,)),
            sem((VARIABLES,)),
            sem((VARIABLES,)),
            sem((VARIABLES,)),
            sem((2,)),
            sem((2,)),
            sem((2,)),
            sem((2, 3)),
            sem((2,)),
            sem((3, 3)),
            sem((3, 3)),
        ],
        compiler_params=pltpu.CompilerParams(
            collective_id=0, has_side_effects=True, vmem_limit_bytes=56 * 1024 * 1024
        ),
    )(
        listed_blocks[0, 0],
        valid_count[0, 0],
        level_kernel[0],
        shaped,
        position[0, 0],
        observations[0, 0],
        precision[0, 0],
    )
    result = pl.pallas_call(
        hand_over,
        out_shape=jax.ShapeDtypeStruct(shaped.shape, jnp.bfloat16),
        in_specs=[whole],
        out_specs=whole,
        scratch_shapes=[pltpu.VMEM(shaped.shape, jnp.bfloat16), sem((8,)), sem((8,))],
        compiler_params=pltpu.CompilerParams(vmem_limit_bytes=56 * 1024 * 1024),
    )(result)
    return result.transpose(0, 2, 1, 3).reshape(ensemble.shape)


def solution(mesh):
    placed = (
        P("member", "patch", None, "level", None, None),
        P("patch", "member", None, None),
        P("patch", "member", None, None),
        P("patch", "member", None),
        P("patch", "member", None, None),
        P("level", None),
        P("patch", "member", None),
    )
    return jax.shard_map(
        body,
        mesh=mesh,
        in_specs=placed,
        out_specs=P("member", "patch", None, "level", None, None),
        check_vma=False,
    )
```
